128 devices in a mesh: dp: 64 (over y, z, x), mp: 2 (over core).
Axes of the slice: x: 4, y: 4, z: 4, core: 2. Of those that a mesh axis runs over, the one named last changes fastest.
Arguments:
- embeddings: bfloat16 [8192, 512], P('dp'), may hold values from -6 to 6
- labels: int32 [8192], replicated, may hold values from 0 to 1048575, as said below
- centres: bfloat16 [1048576, 512], P(('dp', 'mp')), may hold values from -6 to 6
- momentum: bfloat16 [1048576, 512], P(('dp', 'mp')), may hold values from -6 to 6
- sample_rows: int32 [98304], P(('dp', 'mp')), may hold values from 0 to 8191, as said below
- cotangent: float32 [8192], replicated, may hold values from 0.5 to 1.5
Outputs:
- loss: float32 [8192], P('dp')
- grad_embed: float32 [8192, 512], P('dp')
- velocity: float32 [98304, 512], P(('dp', 'mp'))
- new_rows: bfloat16 [98304, 512], P(('dp', 'mp'))
The draws below stay inside these ranges and needn't reach their ends.
Inputs may be any that keep to these rules, and one draw needn't show every extreme that they name: `labels`: each class shard is the label of exactly 64 faces. `sample_rows`: the 768 entries of shard g are distinct rows of that shard's centres and include the row of every face label in shard g.
All inputs are finite; a program needn't handle non-finite values.
Results may differ from the reference program's by a relative error of at most 0.0068.
Values may be sent and summed in bfloat16 or wider, within the bound.
No kernel may reach another device: no remote copies, remote signals or barrier semaphores. Data moves between devices by JAX's collectives and lax.ppermute only.
A program may use at most 192 MiB of HBM per device.

```python
import jax
import jax.numpy as jnp
from jax import lax

D = 512
CLS_DEV = 8192
SAMPLE = 768
TOKENS = 8192
CLASSES = 1048576
SAMPLED = 98304
DEVICES = 128


def shared_faces(key):
    key_order, key_local = jax.random.split(key)
    face_order = jax.random.permutation(key_order, TOKENS)
    owner_shard = face_order % DEVICES
    local_rows = jax.random.randint(key_local, (TOKENS,), 0, CLS_DEV)
    local_rows = jnp.where(face_order == 0, 0, local_rows)
    local_rows = jnp.where(face_order == TOKENS - 1, CLS_DEV - 1, local_rows)
    return (owner_shard.astype(jnp.int32), local_rows.astype(jnp.int32))


def draw_labels(key, part):
    owner_shard, local_rows = shared_faces(key)
    return (owner_shard * CLS_DEV + local_rows).astype(jnp.int32)


def draw_sample_rows(key, part):
    owner_shard, local_rows = shared_faces(key)
    key = jax.random.fold_in(key, 5)
    shard_keys = jax.random.split(key, DEVICES)
    ranks = jax.vmap(lambda single: jax.random.permutation(single, CLS_DEV))(shard_keys)
    marks = jnp.zeros((DEVICES, CLS_DEV), jnp.int32).at[owner_shard, local_rows].set(1)
    scores = ranks.astype(jnp.int32) + CLS_DEV * marks
    chosen = lax.top_k(scores, SAMPLE)[1]
    return chosen.reshape(-1).astype(jnp.int32)


def steps_of(stream_key, extent, pieces, low, largest):
    def one(axis_at, parts):
        heights = jax.random.uniform(jax.random.fold_in(jax.random.fold_in(stream_key, 6), axis_at), (parts,), jnp.float32, low / len(pieces), largest / len(pieces))
        return jnp.repeat(jnp.exp(heights), extent[axis_at] // parts).reshape((-1,) + (1,) * (len(extent) - axis_at - 1))

    factor_of = one(*pieces[0])
    for cut in pieces[1:]:
        factor_of = factor_of * one(*cut)
    return factor_of


def normal_values(own_key, dims, width, bound, pieces=(), held_as=jnp.bfloat16):
    values = width * jax.random.normal(own_key, dims, jnp.float32)
    if pieces:
        values = values * steps_of(own_key, dims, pieces, -0.22, 0.18)
    return jnp.clip(values, -bound, bound).astype(held_as)


def setup_inputs(seed: int = 0) -> dict:
    arg_keys = jax.random.split(jax.random.key(seed), 7)
    embeddings = normal_values(arg_keys[0], (TOKENS, D), 1.0, 6.0, ((0, 64),))
    labels = draw_labels(jax.random.fold_in(arg_keys[6], 71), 0)
    centres = normal_values(arg_keys[2], (CLASSES, D), 1.0, 6.0, ((0, 128),))
    momentum = normal_values(arg_keys[3], (CLASSES, D), 1.0, 6.0, ((0, 128),))
    sample_rows = draw_sample_rows(jax.random.fold_in(arg_keys[6], 71), 0)
    cotangent = jnp.clip(jax.random.uniform(arg_keys[5], (TOKENS,), jnp.float32, 0.5, 1.5), 0.5, 1.5)
    return dict(embeddings=embeddings, labels=labels, centres=centres, momentum=momentum, sample_rows=sample_rows, cotangent=cotangent)


logit_scale = 64.0
cos_margin = 0.8775825618903728
sin_margin = 0.479425538604203
momentum_rate = 0.9
learn_rate = 0.1

def normalize(matrix):
    values = matrix.astype(jnp.float32)
    inverse = lax.rsqrt(lax.optimization_barrier(jnp.sum(values * values, axis=1, keepdims=True)) + 1e-06)
    return (values * inverse, inverse)

def margin_terms(unit_faces, unit_rows, picked_rows, label_owner, label_local, shard_index):
    cosine = lax.dot_general(unit_faces, unit_rows, (((1,), (1,)), ((), ())), preferred_element_type=jnp.float32)
    target = (label_owner == shard_index)[:, None] & (label_local[:, None] == picked_rows[None, :])
    sine_root = jnp.sqrt(1.001 - cosine * cosine)
    shifted = jnp.where(target, cosine * cos_margin - sine_root * sin_margin, cosine)
    return (cosine, target, sine_root, logit_scale * shifted)

def reference(embeddings, labels, centres, momentum, sample_rows, cotangent):
    unit32, inv_emb = normalize(embeddings)
    unit_faces = unit32.astype(jnp.bfloat16)
    label_owner = labels // CLS_DEV
    label_local = labels % CLS_DEV
    blocks = centres.reshape(DEVICES, CLS_DEV, D)
    mom_blocks = momentum.reshape(DEVICES, CLS_DEV, D)
    picks_all = sample_rows.reshape(DEVICES, SAMPLE)
    shard_list = jnp.arange(DEVICES, dtype=jnp.int32)

    def shard_terms(shard_index):
        picked_rows = picks_all[shard_index]
        picked = jnp.take(blocks[shard_index], picked_rows, axis=0)
        rows32, inv_rows = normalize(picked)
        terms = margin_terms(unit_faces, rows32.astype(jnp.bfloat16), picked_rows, label_owner, label_local, shard_index)
        return (picked_rows, picked, rows32, inv_rows, terms)

    def first_pass(running, shard_index):
        picked_rows, picked, rows32, inv_rows, terms = shard_terms(shard_index)
        cosine, target, sine_root, logits = terms
        totals, target_sum = running
        totals = totals + lax.optimization_barrier(jnp.sum(jnp.exp(logits), axis=1))
        target_sum = target_sum + lax.optimization_barrier(jnp.sum(jnp.where(target, logits, 0.0), axis=1))
        return ((totals, target_sum), None)
    zeros_rows = jnp.zeros((TOKENS,), jnp.float32)
    (totals, target_sum), _ = lax.scan(first_pass, (zeros_rows, zeros_rows), shard_list)
    loss = jnp.log(totals) - target_sum
    inv_total = 1.0 / totals

    def second_pass(face_sum, shard_index):
        picked_rows, picked, rows32, inv_rows, terms = shard_terms(shard_index)
        cosine, target, sine_root, logits = terms
        probability = jnp.exp(logits) * inv_total[:, None]
        chain_slope = jnp.where(target, logit_scale * (cos_margin + sin_margin * cosine / sine_root), logit_scale)
        dcos = (cotangent[:, None] * (probability - target.astype(jnp.float32)) * chain_slope).astype(jnp.bfloat16)
        unit_rows = rows32.astype(jnp.bfloat16)
        face_sum = face_sum + jnp.dot(dcos, unit_rows, preferred_element_type=jnp.float32)
        centre_grad = lax.dot_general(dcos, unit_faces, (((0,), (0,)), ((), ())), preferred_element_type=jnp.float32)
        row_grad = inv_rows * (centre_grad - rows32 * lax.optimization_barrier(jnp.sum(rows32 * centre_grad, axis=1, keepdims=True)))
        mom_rows = jnp.take(mom_blocks[shard_index], picked_rows, axis=0)
        velocity = momentum_rate * mom_rows.astype(jnp.float32) + row_grad
        new_rows = (picked.astype(jnp.float32) - learn_rate * velocity).astype(jnp.bfloat16)
        return (face_sum, (velocity, new_rows))
    face_sum, (velocity, new_rows) = lax.scan(second_pass, jnp.zeros((TOKENS, D), jnp.float32), shard_list)
    grad_embed = inv_emb * (face_sum - unit32 * lax.optimization_barrier(jnp.sum(unit32 * face_sum, axis=1, keepdims=True)))
    return (loss, grad_embed, velocity.reshape(SAMPLED, D), new_rows.reshape(SAMPLED, D))
```

```python
import functools

import jax
import jax.numpy as jnp
from jax import lax
from jax.experimental import pallas as pl
from jax.experimental.pallas import tpu as pltpu
from jax.sharding import Mesh
from jax.sharding import PartitionSpec as P

logit_scale = 64.0
cos_margin = 0.8775825618903728
sin_margin = 0.479425538604203
momentum_rate = 0.9
learn_rate = 0.1
exp2_scale = 64.0 * 1.4426950408889634

D = 512
SAMPLE = 768
TAIL = 16
MSG = SAMPLE + TAIL
FACES = 1024
CLS_DEV = 8192
bf16 = jnp.bfloat16
f32 = jnp.float32
VMEM = pl.BlockSpec(memory_space=pltpu.VMEM)


def params(mib):
    return pltpu.CompilerParams(vmem_limit_bytes=mib * 1024 * 1024)


def cost(flops, bytes_accessed, transcendentals=0):
    return pl.CostEstimate(
        flops=flops, bytes_accessed=bytes_accessed, transcendentals=transcendentals
    )


def inverse_norm(values):
    return lax.rsqrt(jnp.sum(values * values, axis=1, keepdims=True) + 1e-06)


def unit_faces_kernel(core_ref, emb_ref, out_ref):
    values = emb_ref[...].astype(f32)
    out_ref[...] = (values * inverse_norm(values)).astype(bf16)


def unit_faces(embeddings, core):
    return pl.pallas_call(
        unit_faces_kernel,
        grid_spec=pltpu.PrefetchScalarGridSpec(
            num_scalar_prefetch=1,
            grid=(1,),
            in_specs=[pl.BlockSpec((64, D), lambda i, core: (core[0], 0))],
            out_specs=pl.BlockSpec((64, D), lambda i, core: (0, 0)),
        ),
        out_shape=jax.ShapeDtypeStruct((64, D), bf16),
        compiler_params=params(16),
        cost_estimate=cost(64 * D * 4, 64 * D * 4),
    )(core, embeddings)


def rows_message_kernel(picked_ref, ids_ref, out_ref, tail_ref):
    values = picked_ref[...].astype(f32)
    out_ref[0:SAMPLE, :] = (values * inverse_norm(values)).astype(bf16)
    ids = ids_ref[...]
    high = ids >> 6
    tail_ref[...] = jnp.zeros_like(tail_ref)
    tail_ref[0:6, 0:128] = high.astype(f32)
    tail_ref[6:12, 0:128] = (ids - high * 64).astype(f32)
    out_ref[SAMPLE:MSG, :] = tail_ref[...].astype(bf16)


def rows_message(picked, ids):
    return pl.pallas_call(
        rows_message_kernel,
        in_specs=[VMEM, VMEM],
        out_specs=VMEM,
        out_shape=jax.ShapeDtypeStruct((MSG, D), bf16),
        scratch_shapes=[pltpu.VMEM((TAIL, D), f32)],
        compiler_params=params(16),
        cost_estimate=cost(SAMPLE * D * 4, SAMPLE * D * 4),
    )(picked, ids.reshape(6, 128))


def exp_kernel(shards_ref, own_ref, mate_ref, faces_ref, labels_ref, before_ref, exp_ref, sums_ref, acc_ref):
    step = pl.program_id(0)

    @pl.when(step == 0)
    def _():
        acc_ref[...] = jnp.zeros_like(acc_ref)

    def block(rows_ref, shard):
        base = (shard * CLS_DEV).astype(f32)
        tail = rows_ref[SAMPLE:MSG, 0:128].astype(f32)
        columns = []
        for b in range(6):
            ids = tail[b : b + 1] * 64.0 + tail[6 + b : 7 + b]
            columns.append(jnp.broadcast_to(ids, (128, 128)).T)
        rows = rows_ref[0:SAMPLE, :]
        for chunk in range(4):
            cosine = lax.dot_general(
                rows,
                faces_ref[chunk * 256 : chunk * 256 + 256, :],
                (((1,), (1,)), ((), ())),
                preferred_element_type=f32,
            )
            for half in range(2):
                lanes = slice(chunk * 256 + half * 128, chunk * 256 + half * 128 + 128)
                wanted = labels_ref[0:1, lanes] - base
                total = acc_ref[0:8, lanes]
                at_target = acc_ref[8:16, lanes]
                for b in range(6):
                    cos = cosine[b * 128 : b * 128 + 128, half * 128 : half * 128 + 128]
                    hit = columns[b] == wanted
                    expo = jnp.where(hit, 0.0, jnp.exp2(cos * exp2_scale))
                    exp_ref[b * 128 : b * 128 + 128, lanes] = expo.astype(bf16)
                    total = total + jnp.sum(expo.reshape(16, 8, 128), axis=0)
                    at_target = at_target + jnp.sum(
                        jnp.where(hit, cos, 0.0).reshape(16, 8, 128), axis=0
                    )
                acc_ref[0:8, lanes] = total
                acc_ref[8:16, lanes] = at_target

    @pl.when(step == 0)
    def _():
        block(own_ref, shards_ref[0])

    @pl.when(step == 1)
    def _():
        block(mate_ref, shards_ref[1])
        sums_ref[0:1, :] = before_ref[0:1, :] + jnp.sum(acc_ref[0:8, :], axis=0, keepdims=True)
        sums_ref[1:2, :] = before_ref[1:2, :] + jnp.sum(acc_ref[8:16, :], axis=0, keepdims=True)


def exp_block(shards, own, mate, faces, labels, before):
    def whole(shape):
        return pl.BlockSpec(shape, lambda i, s: (0, 0))

    return pl.pallas_call(
        exp_kernel,
        grid_spec=pltpu.PrefetchScalarGridSpec(
            num_scalar_prefetch=1,
            grid=(2,),
            in_specs=[
                whole((MSG, D)),
                whole((MSG, D)),
                whole((FACES, D)),
                whole((1, FACES)),
                whole((2, FACES)),
            ],
            out_specs=[pl.BlockSpec((SAMPLE, FACES), lambda i, s: (i, 0)), whole((2, FACES))],
            scratch_shapes=[pltpu.VMEM((16, FACES), f32)],
        ),
        out_shape=[
            jax.ShapeDtypeStruct((2 * SAMPLE, FACES), bf16),
            jax.ShapeDtypeStruct((2, FACES), f32),
        ],
        compiler_params=params(32),
        cost_estimate=cost(
            2 * 2 * SAMPLE * FACES * D, 6 * 1024 * 1024, 2 * SAMPLE * FACES
        ),
    )(shards, own, mate, faces, labels, before)


def grad_kernel(last, exp_ref, own_ref, mate_ref, faces_ref, sums_ref, weight_ref, before_ref, cg_own_ref, cg_mate_ref, out_ref, *scratch):
    step = pl.program_id(0)
    if last:
        dcos_ref, sum_ref = scratch
    else:
        (dcos_ref,) = scratch
        sum_ref = out_ref
    others = sums_ref[0:1, :]
    cos_t = sums_ref[1:2, :]
    sine_root = jnp.sqrt(1.001 - cos_t * cos_t)
    logit_t = logit_scale * (cos_t * cos_margin - sine_root * sin_margin)
    scaled = weight_ref[...] / (others + jnp.exp(logit_t))
    slope = logit_scale * (cos_margin + sin_margin * cos_t / sine_root)
    target_coef = -scaled * others * slope
    coef = scaled * logit_scale

    for chunk in range(8):
        lanes = slice(chunk * 128, chunk * 128 + 128)
        expo = exp_ref[:, lanes].astype(f32)
        dcos_ref[:, lanes] = jnp.where(
            expo == 0.0, target_coef[:, lanes], expo * coef[:, lanes]
        ).astype(bf16)

    def block(rows_ref, cg_ref, first):
        cg_ref[...] = jnp.dot(
            dcos_ref[...], faces_ref[...], preferred_element_type=f32
        ).astype(bf16)
        part = lax.dot_general(
            rows_ref[0:SAMPLE, :],
            dcos_ref[...],
            (((0,), (0,)), ((), ())),
            preferred_element_type=f32,
        )
        sum_ref[...] = (before_ref if first else sum_ref)[...] + part

    @pl.when(step == 0)
    def _():
        block(own_ref, cg_own_ref, True)

    @pl.when(step == 1)
    def _():
        block(mate_ref, cg_mate_ref, False)
        if last:
            out_ref[...] = sum_ref[...].T.astype(bf16)


def grad_block(expo, own, mate, faces, sums, weight, before, last=False):
    def whole(shape):
        return pl.BlockSpec(shape, lambda i: (0, 0))

    return pl.pallas_call(
        functools.partial(grad_kernel, last),
        grid=(2,),
        in_specs=[
            pl.BlockSpec((SAMPLE, FACES), lambda i: (i, 0)),
            whole((MSG, D)),
            whole((MSG, D)),
            whole((FACES, D)),
            whole((2, FACES)),
            whole((1, FACES)),
            whole((D, FACES)),
        ],
        out_specs=[
            whole((SAMPLE, D)),
            whole((SAMPLE, D)),
            whole((FACES, D) if last else (D, FACES)),
        ],
        out_shape=[
            jax.ShapeDtypeStruct((SAMPLE, D), bf16),
            jax.ShapeDtypeStruct((SAMPLE, D), bf16),
            jax.ShapeDtypeStruct((FACES, D), bf16)
            if last
            else jax.ShapeDtypeStruct((D, FACES), f32),
        ],
        scratch_shapes=[pltpu.VMEM((SAMPLE, FACES), bf16)]
        + ([pltpu.VMEM((D, FACES), f32)] if last else []),
        compiler_params=params(40),
        cost_estimate=cost(4 * 2 * SAMPLE * FACES * D, 12 * 1024 * 1024),
    )(expo, own, mate, faces, sums, weight, before)


def rows_end_kernel(picked_ref, mom_ref, a_ref, b_ref, c_ref, d_ref, e_ref, velocity_ref, new_ref):
    picked = picked_ref[...].astype(f32)
    inverse = inverse_norm(picked)
    rows32 = picked * inverse
    grad = (
        a_ref[...].astype(f32)
        + b_ref[...].astype(f32)
        + c_ref[...].astype(f32)
        + d_ref[...].astype(f32)
        + e_ref[...].astype(f32)
    )
    row_grad = inverse * (grad - rows32 * jnp.sum(rows32 * grad, axis=1, keepdims=True))
    velocity = momentum_rate * mom_ref[...].astype(f32) + row_grad
    velocity_ref[...] = velocity
    new_ref[...] = (picked - learn_rate * velocity).astype(bf16)


def rows_end(*arrays):
    spec = pl.BlockSpec((256, D), lambda i: (i, 0))
    return pl.pallas_call(
        rows_end_kernel,
        grid=(3,),
        in_specs=[spec] * 7,
        out_specs=[spec] * 2,
        out_shape=[
            jax.ShapeDtypeStruct((SAMPLE, D), f32),
            jax.ShapeDtypeStruct((SAMPLE, D), bf16),
        ],
        compiler_params=params(16),
        cost_estimate=cost(SAMPLE * D * 20, SAMPLE * D * 20),
    )(*arrays)


def faces_end_kernel(core_ref, emb_ref, a_ref, b_ref, c_ref, d_ref, out_ref):
    values = emb_ref[...].astype(f32)
    inverse = inverse_norm(values)
    unit = values * inverse
    summed = (
        a_ref[...].astype(f32)
        + b_ref[...].astype(f32)
        + c_ref[...].astype(f32)
        + d_ref[...].astype(f32)
    )
    out_ref[...] = inverse * (summed - unit * jnp.sum(unit * summed, axis=1, keepdims=True))


def faces_end(embeddings, core, parts):
    spec = pl.BlockSpec((64, D), lambda i, core: (0, 0))
    return pl.pallas_call(
        faces_end_kernel,
        grid_spec=pltpu.PrefetchScalarGridSpec(
            num_scalar_prefetch=1,
            grid=(1,),
            in_specs=[pl.BlockSpec((64, D), lambda i, core: (core[0], 0))] + [spec] * 4,
            out_specs=spec,
        ),
        out_shape=jax.ShapeDtypeStruct((64, D), f32),
        compiler_params=params(16),
        cost_estimate=cost(64 * D * 12, 64 * D * 16),
    )(core, embeddings, *parts)


def shift(array, axis, k):
    return lax.ppermute(array, axis, [((i + k) % 4, i) for i in range(4)])


def swap(array):
    return lax.ppermute(array, "core", [(0, 1), (1, 0)])


def gather(array, axis):
    here = lax.axis_index(axis)
    size = array.shape[0]
    whole = jnp.zeros((4 * size,) + array.shape[1:], array.dtype)
    for k in (0, 2, 1, 3):
        part = shift(array, axis, k) if k else array
        whole = lax.dynamic_update_slice_in_dim(whole, part, ((here + k) % 4) * size, 0)
    return whole


def total(array, axis):
    return array + shift(array, axis, 2) + shift(array, axis, 1) + shift(array, axis, 3)


def scatter_parts(array, axis):
    here = lax.axis_index(axis)
    size = array.shape[0] // 4

    def piece(k):
        return lax.dynamic_slice_in_dim(array, ((here + k) % 4) * size, size, 0)

    return [piece(0)] + [shift(piece(k), axis, -k) for k in (2, 1, 3)]


def shards(embeddings, labels, centres, momentum, sample_rows, cotangent):
    y, z, x, core = (lax.axis_index(name) for name in ("y", "z", "x", "core"))
    core1 = core.reshape(1).astype(jnp.int32)

    def mine(array):
        picked = array.reshape(16, 4, 2, 64)
        picked = lax.dynamic_slice(picked, (0, x, core, 0), (16, 1, 1, 64))
        return picked.reshape(1, FACES).astype(f32)

    my_labels = mine(labels)
    weight = mine(cotangent)

    unit = unit_faces(embeddings, core1)
    picked = centres.at[sample_rows].get(mode="promise_in_bounds", unique_indices=True)
    message = rows_message(picked, sample_rows)

    faces = gather(gather(unit, "z"), "y")

    order = (0, 1, 3, 2)
    own_rows = {k: shift(message, "x", k) if k else message for k in (0, 1, 3, 2)}
    mate_rows = {k: swap(own_rows[k]) for k in order}

    def shard_pair(k):
        first = ((y * 16 + z * 4 + (x + k) % 4) * 2).astype(jnp.int32)
        return jnp.stack([first + core, first + 1 - core]).astype(jnp.int32)

    sums = jnp.zeros((2, FACES), f32)
    expo = {}
    for k in order:
        expo[k], sums = exp_block(
            shard_pair(k), own_rows[k], mate_rows[k], faces, my_labels, sums
        )
    sums = total(total(sums, "y"), "z")

    mom_rows = momentum.at[sample_rows].get(mode="promise_in_bounds", unique_indices=True)

    cos_t = sums[1]
    logit_t = logit_scale * (cos_t * cos_margin - jnp.sqrt(1.001 - cos_t * cos_t) * sin_margin)
    full_loss = jnp.log(sums[0] + jnp.exp(logit_t)) - logit_t
    half_loss = lax.dynamic_slice_in_dim(full_loss, (y * 4 + z) * 64, 64, 0)

    face_sum = jnp.zeros((D, FACES), f32)
    arrived = []
    own_parts = None
    for k in (2, 1, 3, 0):
        cg_own, cg_mate, face_sum = grad_block(
            expo[k], own_rows[k], mate_rows[k], faces, sums, weight, face_sum, last=(k == 0)
        )
        from_mate = swap(cg_mate)
        if k:
            both = (cg_own.astype(f32) + from_mate.astype(f32)).astype(bf16)
            arrived.append(shift(both, "x", -k))
        else:
            own_parts = (cg_own, from_mate)

    parts = scatter_parts(face_sum, "y")
    summed = parts[0].astype(f32)
    for part in parts[1:]:
        summed = summed + part.astype(f32)
    parts = scatter_parts(summed.astype(bf16), "z")
    half_grad = faces_end(embeddings, core1, parts)

    velocity, new_rows = rows_end(picked, mom_rows, *own_parts, *arrived)

    def both_halves(half):
        other = swap(half)
        return jnp.where(
            core == 0,
            jnp.concatenate([half, other], axis=0),
            jnp.concatenate([other, half], axis=0),
        )

    return (both_halves(half_loss), both_halves(half_grad), velocity, new_rows)


def solution(mesh):
    grid = Mesh(mesh.devices.reshape(4, 4, 4, 2), ("y", "z", "x", "core"))
    chips = ("y", "z", "x")
    devices = ("y", "z", "x", "core")
    return jax.shard_map(
        shards,
        mesh=grid,
        in_specs=(
            P(chips, None),
            P(),
            P(devices, None),
            P(devices, None),
            P(devices),
            P(),
        ),
        out_specs=(P(chips), P(chips, None), P(devices, None), P(devices, None)),
        check_vma=False,
    )
```

```python
import functools

import jax
import jax.numpy as jnp
from jax import lax
from jax.experimental import pallas as pl
from jax.experimental.pallas import tpu as pltpu
from jax.sharding import Mesh
from jax.sharding import PartitionSpec as P

logit_scale = 64.0
cos_margin = 0.8775825618903728
sin_margin = 0.479425538604203
momentum_rate = 0.9
learn_rate = 0.1
exp2_scale = 64.0 * 1.4426950408889634

D = 512
SAMPLE = 768
TAIL = 16
HALF = SAMPLE // 2
PART = HALF + TAIL
MSG = 2 * PART
FACES = 1024
CLS_DEV = 8192
bf16 = jnp.bfloat16
f32 = jnp.float32
VMEM = pl.BlockSpec(memory_space=pltpu.VMEM)
HBM = pl.BlockSpec(memory_space=pltpu.HBM)
ANY = pl.BlockSpec(memory_space=pl.ANY)
SMEM = pl.BlockSpec(memory_space=pltpu.SMEM)


def params(mib):
    return pltpu.CompilerParams(vmem_limit_bytes=mib * 1024 * 1024)


def cost(flops, bytes_accessed, transcendentals=0):
    return pl.CostEstimate(
        flops=flops // 16, bytes_accessed=bytes_accessed // 16, transcendentals=transcendentals // 16
    )


def inverse_norm(values):
    return lax.rsqrt(jnp.sum(values * values, axis=1, keepdims=True) + 1e-06)


def here(axis):
    return lax.axis_index(axis).astype(jnp.int32)


def tie(array, *others):
    def nothing(*refs):
        pass

    return pl.pallas_call(
        nothing,
        in_specs=[ANY] * (1 + len(others)),
        out_specs=ANY,
        out_shape=jax.ShapeDtypeStruct(array.shape, array.dtype),
        input_output_aliases={0: 0},
        compiler_params=params(1),
    )(array, *others)


def my_faces(table_ref, out_ref):
    x, core = here("x"), here("core")
    lane = lax.broadcasted_iota(jnp.int32, (1, 128), 1)
    for pair in range(8):
        left = table_ref[pl.ds(pair * 8 + x, 1), :].astype(f32)
        right = table_ref[pl.ds(pair * 8 + 4 + x, 1), :].astype(f32)
        left = jnp.where(core == 0, left, pltpu.roll(left, 64, 1))
        right = jnp.where(core == 0, pltpu.roll(right, 64, 1), right)
        out_ref[:, pair * 128 : pair * 128 + 128] = jnp.where(lane < 64, left, right)


def prepare_kernel(picked_ref, ids_ref, emb_ref, labels_ref, weight_ref, out_ref, unit_ref, my_labels_ref, my_weight_ref, tail_ref):
    start = pl.multiple_of(here("core") * 64, 64)
    values = emb_ref[pl.ds(start, 64), :].astype(f32)
    unit_ref[...] = (values * inverse_norm(values)).astype(bf16)
    ids = ids_ref[...]
    high = (ids >> 6).astype(f32)
    low = (ids & 63).astype(f32)
    for half in range(2):
        values = picked_ref[half * HALF : half * HALF + HALF, :].astype(f32)
        at = half * PART
        out_ref[at : at + HALF, :] = (values * inverse_norm(values)).astype(bf16)
        tail_ref[...] = jnp.zeros_like(tail_ref)
        tail_ref[0:3, 0:128] = high[half * 3 : half * 3 + 3]
        tail_ref[3:6, 0:128] = low[half * 3 : half * 3 + 3]
        out_ref[at + HALF : at + PART, :] = tail_ref[...].astype(bf16)
    my_faces(labels_ref, my_labels_ref)
    my_faces(weight_ref, my_weight_ref)


def cut_kernel(half, array_ref, out_ref):
    out_ref[...] = array_ref[half * PART : half * PART + PART, :]


def cut(half, message):
    return pl.pallas_call(
        functools.partial(cut_kernel, half),
        in_specs=[VMEM],
        out_specs=VMEM,
        out_shape=jax.ShapeDtypeStruct((PART, D), bf16),
        compiler_params=params(2),
        cost_estimate=cost(0, PART * D * 4),
    )(message)


def prepare(picked, ids, embeddings, labels, cotangent):
    return pl.pallas_call(
        prepare_kernel,
        in_specs=[VMEM] * 5,
        out_specs=[VMEM] * 4,
        out_shape=[
            jax.ShapeDtypeStruct((MSG, D), bf16),
            jax.ShapeDtypeStruct((64, D), bf16),
            jax.ShapeDtypeStruct((1, FACES), f32),
            jax.ShapeDtypeStruct((1, FACES), f32),
        ],
        scratch_shapes=[pltpu.VMEM((TAIL, D), f32)],
        compiler_params=params(8),
        cost_estimate=cost(SAMPLE * D * 4, SAMPLE * D * 4),
    )(picked, ids.reshape(6, 128), embeddings, labels.reshape(64, 128), cotangent.reshape(64, 128))


def assemble_kernel(*refs):
    out_ref, token_ref = refs[-2:]
    size = refs[0].shape[0]
    for k, ref in enumerate(refs[:4]):
        at = pl.multiple_of(lax.rem(here("z") + k, 4) * size, size)
        out_ref[pl.ds(at, size), :] = ref[...]
    token_ref[...] = jnp.zeros_like(token_ref)


def assemble(parts):
    size = parts[0].shape[0]
    return pl.pallas_call(
        assemble_kernel,
        in_specs=[VMEM] * 4,
        out_specs=[VMEM] * 2,
        out_shape=[
            jax.ShapeDtypeStruct((4 * size, D), bf16),
            jax.ShapeDtypeStruct((8, 128), f32),
        ],
        compiler_params=params(8),
        cost_estimate=cost(0, size * D * 16),
    )(*parts)


def row_parts(refs):
    if len(refs) == 2:
        return [(ref, at) for ref in refs for at in (0, PART)]
    return [(ref, 0) for ref in refs]


def exp_kernel(below, far, n_rows, *refs):
    parts = row_parts(refs[:n_rows])
    f0, f1, f2, f3, labels_ref = refs[n_rows : n_rows + 5]
    refs = refs[n_rows + 5 :]
    exp_ref, sums_ref = refs[-2:]
    x, y, core = here("x"), here("y"), here("core")
    line = y * 16 + here("z") * 4
    first = (line + lax.rem(x + 4 - below, 4)) * 2
    second = (line + lax.rem(x + 4 - (4 - below if far else below), 4)) * 2
    numbers = (first + core, second + core, first + 1 - core, second + 1 - core)
    places = [
        pl.ds(pl.multiple_of(lax.rem(y + chunk, 4) * 256, 256), 256) for chunk in range(4)
    ]
    totals = [None] * 8
    at_targets = [None] * 8
    for part, (rows_ref, at_row) in enumerate(parts):
        base = (numbers[part] * CLS_DEV).astype(f32)
        tail = rows_ref[at_row + HALF : at_row + PART, 0:128].astype(f32)
        columns = []
        for b in range(3):
            ids = tail[b : b + 1] * 64.0 + tail[3 + b : 4 + b] + base
            columns.append(jnp.broadcast_to(ids, (128, 128)).T)
        for chunk, faces_ref in enumerate((f0, f1, f2, f3)):
            cosine = lax.dot_general(
                rows_ref[at_row : at_row + HALF, :],
                faces_ref[...],
                (((1,), (1,)), ((), ())),
                preferred_element_type=f32,
            )
            labels = labels_ref[0:1, places[chunk]]
            for half in range(2):
                lane = chunk * 2 + half
                lanes = slice(lane * 128, lane * 128 + 128)
                wanted = labels[:, half * 128 : half * 128 + 128]
                total, at_target = totals[lane], at_targets[lane]
                for b in range(3):
                    cos = cosine[b * 128 : b * 128 + 128, half * 128 : half * 128 + 128]
                    hit = columns[b] == wanted
                    expo = jnp.where(hit, 0.0, jnp.exp2(cos * exp2_scale))
                    at = part * HALF + b * 128
                    exp_ref[at : at + 128, lanes] = expo.astype(bf16)
                    expo = jnp.sum(expo.reshape(16, 8, 128), axis=0)
                    chosen = jnp.sum(jnp.where(hit, cos, 0.0).reshape(16, 8, 128), axis=0)
                    total = expo if total is None else total + expo
                    at_target = chosen if at_target is None else at_target + chosen
                totals[lane], at_targets[lane] = total, at_target
    for chunk in range(4):
        for row, found in ((0, totals), (1, at_targets)):
            both = jnp.concatenate([found[2 * chunk], found[2 * chunk + 1]], axis=1)
            value = jnp.sum(both, axis=0, keepdims=True)
            if below:
                value = value + refs[0][row : row + 1, places[chunk]]
            sums_ref[row : row + 1, places[chunk]] = value


def exp_block(below, rows, faces, labels, *others):
    return pl.pallas_call(
        functools.partial(exp_kernel, below, below == 2, len(rows)),
        in_specs=[VMEM] * (5 + len(rows) + (len(others) if below else 0)) + ([] if below else [ANY] * len(others)),
        out_specs=[VMEM] * 2,
        out_shape=[
            jax.ShapeDtypeStruct((4 * HALF, FACES), bf16),
            jax.ShapeDtypeStruct((2, FACES), f32),
        ],
        compiler_params=params(8),
        cost_estimate=cost(0, 0),
    )(*rows, *faces, labels, *others)


def grad_kernel(first, last, n_after, n_rows, exp_ref, *refs):
    parts = row_parts(refs[:n_rows])
    f0, f1, f2, f3, sums_ref, weight_ref = refs[n_rows : n_rows + 6]
    refs = list(refs[n_rows + 6 :])
    before_ref = None if first else refs.pop(0)
    refs = refs[n_after:]
    cg_own_ref, cg_mate_ref = refs[:2]
    outs = refs[2:-2]
    coef_ref, dcos_ref = refs[-2:]
    y = here("y")
    places = [
        pl.ds(pl.multiple_of(lax.rem(y + chunk, 4) * 256, 256), 256) for chunk in range(4)
    ]

    others = sums_ref[0:1, :]
    cos_t = sums_ref[1:2, :]
    sine_root = jnp.sqrt(1.001 - cos_t * cos_t)
    logit_t = logit_scale * (cos_t * cos_margin - sine_root * sin_margin)
    scaled = weight_ref[...] / (others + jnp.exp(logit_t))
    slope = logit_scale * (cos_margin + sin_margin * cos_t / sine_root)
    coef_ref[0:1, :] = scaled * logit_scale
    coef_ref[1:2, :] = -scaled * others * slope
    coef = [coef_ref[0:1, place] for place in places]
    target_coef = [coef_ref[1:2, place] for place in places]

    for part in range(4):
        for chunk in range(4):
            rows = slice(part * HALF, part * HALF + HALF)
            lanes = slice(chunk * 256, chunk * 256 + 256)
            expo = exp_ref[rows, lanes].astype(f32)
            dcos_ref[rows, lanes] = jnp.where(
                expo == 0.0, target_coef[chunk], expo * coef[chunk]
            ).astype(bf16)
        grad = None
        for chunk, faces_ref in enumerate((f0, f1, f2, f3)):
            lanes = slice(chunk * 256, chunk * 256 + 256)
            term = jnp.dot(dcos_ref[rows, lanes], faces_ref[...], preferred_element_type=f32)
            grad = term if grad is None else grad + term
        cg_ref = (cg_own_ref, cg_mate_ref)[part // 2]
        cg_ref[(part % 2) * HALF : (part % 2) * HALF + HALF, :] = grad.astype(bf16)
    for chunk in range(4):
        lanes = slice(chunk * 256, chunk * 256 + 256)
        summed = None if first else before_ref[:, lanes]
        for part, (rows_ref, at_row) in enumerate(parts):
            term = lax.dot_general(
                rows_ref[at_row : at_row + HALF, :],
                dcos_ref[part * HALF : part * HALF + HALF, lanes],
                (((0,), (0,)), ((), ())),
                preferred_element_type=f32,
            )
            summed = term if summed is None else summed + term
        if last:
            outs[chunk][...] = summed.T.astype(bf16)
        else:
            outs[0][:, lanes] = summed


def grad_block(expo, rows, faces, sums, weight, before, last, *after):
    first = before is None
    given = [] if first else [before]
    shapes = [jax.ShapeDtypeStruct((SAMPLE, D), bf16)] * 2
    if last:
        shapes = shapes + [jax.ShapeDtypeStruct((256, D), bf16)] * 4
    else:
        shapes = shapes + [jax.ShapeDtypeStruct((D, FACES), f32)]
    out = pl.pallas_call(
        functools.partial(grad_kernel, first, last, len(after), len(rows)),
        in_specs=[VMEM] * (7 + len(rows) + len(given)) + [ANY] * len(after),
        out_specs=[VMEM] * len(shapes),
        out_shape=shapes,
        scratch_shapes=[pltpu.VMEM((2, FACES), f32), pltpu.VMEM((4 * HALF, FACES), bf16)],
        compiler_params=params(12),
        cost_estimate=cost(0, 0),
    )(expo, *rows, *faces, sums, weight, *given, *after)
    return out[0], out[1], out[2:]


def join_kernel(at, own_ref, mate_ref, *refs):
    out_ref = refs[-1]
    for half in range(2):
        rows = slice(half * HALF, half * HALF + HALF)
        value = own_ref[rows, :].astype(f32) + mate_ref[rows, :].astype(f32)
        if at == half:
            value = value + refs[0][...].astype(f32)
        out_ref[rows, :] = value.astype(bf16)


def join(cg, from_mate, at, arrived, *after):
    return pl.pallas_call(
        functools.partial(join_kernel, at),
        in_specs=[VMEM] * 3 + [ANY] * len(after),
        out_specs=VMEM,
        out_shape=jax.ShapeDtypeStruct((SAMPLE, D), bf16),
        compiler_params=params(8),
        cost_estimate=cost(SAMPLE * D * 2, SAMPLE * D * 6),
    )(cg, from_mate, arrived, *after)


def join_halves_kernel(own_ref, mate_ref, *out_refs):
    for half, out_ref in enumerate(out_refs):
        rows = slice(half * HALF, half * HALF + HALF)
        out_ref[...] = (own_ref[rows, :].astype(f32) + mate_ref[rows, :].astype(f32)).astype(bf16)


def join_halves(cg, from_mate):
    return pl.pallas_call(
        join_halves_kernel,
        in_specs=[VMEM] * 2,
        out_specs=[VMEM] * 2,
        out_shape=[jax.ShapeDtypeStruct((HALF, D), bf16)] * 2,
        compiler_params=params(8),
        cost_estimate=cost(SAMPLE * D * 2, SAMPLE * D * 6),
    )(cg, from_mate)


def rows_base_kernel(picked_ref, mom_ref, own_ref, mate_ref, base_ref):
    picked = picked_ref[...].astype(f32)
    inverse = inverse_norm(picked)
    rows32 = picked * inverse
    grad = own_ref[...].astype(f32) + mate_ref[...].astype(f32)
    row_grad = inverse * (grad - rows32 * jnp.sum(rows32 * grad, axis=1, keepdims=True))
    base_ref[...] = momentum_rate * mom_ref[...].astype(f32) + row_grad


def rows_base(*arrays):
    return pl.pallas_call(
        rows_base_kernel,
        in_specs=[VMEM] * 4,
        out_specs=VMEM,
        out_shape=jax.ShapeDtypeStruct((SAMPLE, D), f32),
        compiler_params=params(8),
        cost_estimate=cost(SAMPLE * D * 20, SAMPLE * D * 16),
    )(*arrays)


def rows_end_kernel(picked_ref, base_ref, v0_ref, v1_ref, velocity_ref, new_ref, velocity_buf, new_buf, sem):
    copies = []
    for half in range(2):
        rows = slice(half * HALF, half * HALF + HALF)
        picked = picked_ref[rows, :].astype(f32)
        inverse = inverse_norm(picked)
        rows32 = picked * inverse
        grad = v0_ref[rows, :].astype(f32) + v1_ref[rows, :].astype(f32)
        row_grad = inverse * (grad - rows32 * jnp.sum(rows32 * grad, axis=1, keepdims=True))
        velocity = base_ref[rows, :] + row_grad
        velocity_buf[rows, :] = velocity
        new_buf[rows, :] = (picked - learn_rate * velocity).astype(bf16)
        place = pl.ds(half * HALF, HALF)
        for i, (buf, ref) in enumerate(((velocity_buf, velocity_ref), (new_buf, new_ref))):
            copy = pltpu.make_async_copy(buf.at[place, :], ref.at[place, :], sem.at[half, i])
            copy.start()
            copies.append(copy)
    for copy in copies:
        copy.wait()


def rows_end(*arrays):
    return pl.pallas_call(
        rows_end_kernel,
        in_specs=[VMEM] * 4,
        out_specs=[HBM] * 2,
        out_shape=[
            jax.ShapeDtypeStruct((SAMPLE, D), f32),
            jax.ShapeDtypeStruct((SAMPLE, D), bf16),
        ],
        scratch_shapes=[
            pltpu.VMEM((SAMPLE, D), f32),
            pltpu.VMEM((SAMPLE, D), bf16),
            pltpu.SemaphoreType.DMA((2, 2)),
        ],
        compiler_params=params(8),
        cost_estimate=cost(SAMPLE * D * 20, SAMPLE * D * 16),
    )(*arrays)


def split_kernel(a_ref, b_ref, c_ref, d_ref, *refs):
    for k, out_ref in enumerate(refs[-4:]):
        rows = pl.ds(pl.multiple_of(lax.rem(here("z") + k, 4) * 64, 64), 64)
        out_ref[...] = (
            a_ref[rows, :].astype(f32)
            + b_ref[rows, :].astype(f32)
            + c_ref[rows, :].astype(f32)
            + d_ref[rows, :].astype(f32)
        ).astype(bf16)


def split(parts, *after):
    return pl.pallas_call(
        split_kernel,
        in_specs=[VMEM] * 4 + [ANY] * len(after),
        out_specs=[VMEM] * 4,
        out_shape=[jax.ShapeDtypeStruct((64, D), bf16)] * 4,
        compiler_params=params(8),
        cost_estimate=cost(256 * D * 4, 256 * D * 10),
    )(*parts, *after)


def faces_end_kernel(emb_ref, sums_ref, a_ref, b_ref, c_ref, d_ref, out_ref, loss_ref):
    start = pl.multiple_of(here("core") * 64, 64)
    values = emb_ref[pl.ds(start, 64), :].astype(f32)
    inverse = inverse_norm(values)
    unit = values * inverse
    summed = (
        a_ref[...].astype(f32)
        + b_ref[...].astype(f32)
        + c_ref[...].astype(f32)
        + d_ref[...].astype(f32)
    )
    out_ref[...] = inverse * (summed - unit * jnp.sum(unit * summed, axis=1, keepdims=True))
    block = here("y") * 4 + here("z")
    lanes = pl.ds(pl.multiple_of(lax.div(block, 2) * 128, 128), 128)
    cos_t = sums_ref[1:2, lanes]
    sine_root = jnp.sqrt(1.001 - cos_t * cos_t)
    logit_t = logit_scale * (cos_t * cos_margin - sine_root * sin_margin)
    loss = jnp.log(sums_ref[0:1, lanes] + jnp.exp(logit_t)) - logit_t
    loss_ref[...] = jnp.where(lax.rem(block, 2) == 0, loss, pltpu.roll(loss, 64, 1))


def faces_end(embeddings, sums, parts):
    return pl.pallas_call(
        faces_end_kernel,
        in_specs=[VMEM] * 6,
        out_specs=[VMEM] * 2,
        out_shape=[
            jax.ShapeDtypeStruct((64, D), f32),
            jax.ShapeDtypeStruct((1, 128), f32),
        ],
        compiler_params=params(8),
        cost_estimate=cost(64 * D * 12, 64 * D * 16),
    )(embeddings, sums, *parts)


def both_cores_kernel(grad_ref, mate_grad_ref, loss_ref, mate_loss_ref, out_ref, out_loss_ref):
    core = here("core")
    out_ref[pl.ds(pl.multiple_of(core * 64, 64), 64), :] = grad_ref[...]
    out_ref[pl.ds(pl.multiple_of(64 - core * 64, 64), 64), :] = mate_grad_ref[...]
    lane = lax.broadcasted_iota(jnp.int32, (1, 128), 1)
    low = jnp.where(core == 0, loss_ref[...], mate_loss_ref[...])
    high = jnp.where(core == 0, mate_loss_ref[...], loss_ref[...])
    out_loss_ref[...] = jnp.where(lane < 64, low, pltpu.roll(high, 64, 1))


def both_cores(*arrays):
    return pl.pallas_call(
        both_cores_kernel,
        in_specs=[VMEM] * 4,
        out_specs=[VMEM] * 2,
        out_shape=[
            jax.ShapeDtypeStruct((128, D), f32),
            jax.ShapeDtypeStruct((1, 128), f32),
        ],
        compiler_params=params(8),
        cost_estimate=cost(0, 64 * D * 16),
    )(*arrays)


def shift(array, axis, k):
    return lax.ppermute(array, axis, [((i + k) % 4, i) for i in range(4)])


def swap(array):
    return lax.ppermute(array, "core", [(0, 1), (1, 0)])


def total(array, axis):
    return array + shift(array, axis, 2) + shift(array, axis, 1) + shift(array, axis, 3)


def gather_rows(array, ids):
    return lax.gather(
        array,
        ids[:, None],
        lax.GatherDimensionNumbers(
            offset_dims=(1,), collapsed_slice_dims=(0,), start_index_map=(0,)
        ),
        slice_sizes=(1, D),
        mode=lax.GatherScatterMode.PROMISE_IN_BOUNDS,
    )


def shards(embeddings, labels, centres, momentum, sample_rows, cotangent):
    picked = gather_rows(centres, sample_rows)
    message, unit, my_labels, weight = prepare(
        picked, sample_rows, embeddings, labels, cotangent
    )

    up = shift(message, "x", -1)
    down = shift(message, "x", 1)
    own_rows = [message, swap(message)]

    plane, token = assemble([unit] + [shift(unit, "z", k) for k in (1, 2, 3)])
    faces = [plane] + [shift(plane, "y", k) for k in (1, 2, 3)]

    up, down = tie(up, *faces[1:]), tie(down, *faces[1:])
    c0 = shift(cut(0, up), "x", -1)
    d1 = shift(cut(1, down), "x", 1)

    expo = {}
    expo["own"], sums_own = exp_block(0, own_rows, faces, my_labels)
    up_rows = [up, swap(up)]
    expo["up"], sums_up = exp_block(1, up_rows, faces, my_labels, sums_own)
    down_rows = [down, swap(down)]
    expo["down"], sums_down = exp_block(3, down_rows, faces, my_labels, sums_up)
    c0, d1 = tie(c0, sums_up), tie(d1, sums_up)
    far_rows = [c0, d1, swap(c0), swap(d1)]
    expo["far"], sums = exp_block(2, far_rows, faces, my_labels, sums_down)
    sums = total(total(sums, "y"), "z")

    def grads(name, rows, before, last, *after):
        cg_own, cg_mate, out = grad_block(
            expo[name], rows, faces, sums, weight, before, last, *after
        )
        return cg_own, cg_mate, out

    far_own, far_mate, (face_sum,) = grads("far", far_rows, None, False)
    t0, t1 = join_halves(far_own, swap(far_mate))
    r0, r1 = shift(t0, "x", 1), shift(t1, "x", -1)
    cg_own, cg_mate, (face_sum,) = grads("own", own_rows, face_sum, False, t0)
    cg_mate = swap(cg_mate)
    up_own, up_mate, (face_sum,) = grads("up", up_rows, face_sum, False)
    up_mate = swap(up_mate)
    down_own, down_mate, parts = grads("down", down_rows, face_sum, True, r0, r1, cg_mate)
    down_mate = swap(down_mate)
    v_up = join(up_own, up_mate, 0, r0)
    v_down = join(down_own, down_mate, 1, r1, parts[0])
    v0, v1 = shift(v_up, "x", 1), shift(v_down, "x", -1)

    mom_rows = gather_rows(momentum, tie(sample_rows, v_down))
    parts = split(
        [parts[0]] + [shift(parts[k], "y", -k) for k in (1, 2, 3)], v_up, v_down, mom_rows
    )
    parts = [parts[0]] + [shift(parts[k], "z", -k) for k in (1, 2, 3)]
    base = rows_base(picked, mom_rows, cg_own, cg_mate)
    half_grad, half_loss = faces_end(embeddings, sums, parts)
    grad_embed, loss = both_cores(half_grad, swap(half_grad), half_loss, swap(half_loss))

    velocity, new_rows = rows_end(picked, base, v0, v1)
    return (loss.reshape(128), grad_embed, velocity, new_rows)


def solution(mesh):
    grid = Mesh(mesh.devices.reshape(4, 4, 4, 2), ("y", "z", "x", "core"))
    chips = ("y", "z", "x")
    devices = ("y", "z", "x", "core")
    return jax.shard_map(
        shards,
        mesh=grid,
        in_specs=(
            P(chips, None),
            P(),
            P(devices, None),
            P(devices, None),
            P(devices),
            P(),
        ),
        out_specs=(P(chips), P(chips, None), P(devices, None), P(devices, None)),
        check_vma=False,
    )
```

```python
import functools

import jax
import jax.numpy as jnp
from jax import lax
from jax.experimental import pallas as pl
from jax.experimental.pallas import tpu as pltpu
from jax.sharding import Mesh
from jax.sharding import PartitionSpec as P

logit_scale = 64.0
cos_margin = 0.8775825618903728
sin_margin = 0.479425538604203
momentum_rate = 0.9
learn_rate = 0.1
exp2_scale = 64.0 * 1.4426950408889634

D = 512
SAMPLE = 768
TAIL = 16
HALF = SAMPLE // 2
PART = HALF + TAIL
MSG = 2 * PART
FACES = 1024
CLS_DEV = 8192
bf16 = jnp.bfloat16
f32 = jnp.float32
VMEM = pl.BlockSpec(memory_space=pltpu.VMEM)
HBM = pl.BlockSpec(memory_space=pltpu.HBM)
ANY = pl.BlockSpec(memory_space=pl.ANY)
SMEM = pl.BlockSpec(memory_space=pltpu.SMEM)


def params(mib):
    return pltpu.CompilerParams(vmem_limit_bytes=mib * 1024 * 1024)


def cost(flops, bytes_accessed, transcendentals=0):
    return pl.CostEstimate(
        flops=flops // 16, bytes_accessed=bytes_accessed // 16, transcendentals=transcendentals // 16
    )


def inverse_norm(values):
    return lax.rsqrt(jnp.sum(values * values, axis=1, keepdims=True) + 1e-06)


def here(axis):
    return lax.axis_index(axis).astype(jnp.int32)


def tie(array, *others):
    def nothing(*refs):
        pass

    return pl.pallas_call(
        nothing,
        in_specs=[ANY] * (1 + len(others)),
        out_specs=ANY,
        out_shape=jax.ShapeDtypeStruct(array.shape, array.dtype),
        input_output_aliases={0: 0},
        compiler_params=params(1),
    )(array, *others)


def my_faces(table_ref, out_ref):
    x, core = here("x"), here("core")
    lane = lax.broadcasted_iota(jnp.int32, (1, 128), 1)
    for pair in range(8):
        left = table_ref[pl.ds(pair * 8 + x, 1), :].astype(f32)
        right = table_ref[pl.ds(pair * 8 + 4 + x, 1), :].astype(f32)
        left = jnp.where(core == 0, left, pltpu.roll(left, 64, 1))
        right = jnp.where(core == 0, pltpu.roll(right, 64, 1), right)
        out_ref[:, pair * 128 : pair * 128 + 128] = jnp.where(lane < 64, left, right)


def prepare_kernel(picked_ref, ids_ref, emb_ref, labels_ref, weight_ref, out_ref, unit_ref, my_labels_ref, my_weight_ref, tail_ref):
    start = pl.multiple_of(here("core") * 64, 64)
    values = emb_ref[pl.ds(start, 64), :].astype(f32)
    unit_ref[...] = (values * inverse_norm(values)).astype(bf16)
    ids = ids_ref[...]
    high = (ids >> 6).astype(f32)
    low = (ids & 63).astype(f32)
    for half in range(2):
        values = picked_ref[half * HALF : half * HALF + HALF, :].astype(f32)
        at = half * PART
        out_ref[at : at + HALF, :] = (values * inverse_norm(values)).astype(bf16)
        tail_ref[...] = jnp.zeros_like(tail_ref)
        tail_ref[0:3, 0:128] = high[half * 3 : half * 3 + 3]
        tail_ref[3:6, 0:128] = low[half * 3 : half * 3 + 3]
        out_ref[at + HALF : at + PART, :] = tail_ref[...].astype(bf16)
    my_faces(labels_ref, my_labels_ref)
    my_faces(weight_ref, my_weight_ref)


def cut_kernel(half, array_ref, out_ref):
    out_ref[...] = array_ref[half * PART : half * PART + PART, :]


def cut(half, message):
    return pl.pallas_call(
        functools.partial(cut_kernel, half),
        in_specs=[VMEM],
        out_specs=VMEM,
        out_shape=jax.ShapeDtypeStruct((PART, D), bf16),
        compiler_params=params(2),
        cost_estimate=cost(0, PART * D * 4),
    )(message)


def prepare(picked, ids, embeddings, labels, cotangent):
    return pl.pallas_call(
        prepare_kernel,
        in_specs=[VMEM] * 5,
        out_specs=[VMEM] * 4,
        out_shape=[
            jax.ShapeDtypeStruct((MSG, D), bf16),
            jax.ShapeDtypeStruct((64, D), bf16),
            jax.ShapeDtypeStruct((1, FACES), f32),
            jax.ShapeDtypeStruct((1, FACES), f32),
        ],
        scratch_shapes=[pltpu.VMEM((TAIL, D), f32)],
        compiler_params=params(8),
        cost_estimate=cost(SAMPLE * D * 4, SAMPLE * D * 4),
    )(picked, ids.reshape(6, 128), embeddings, labels.reshape(64, 128), cotangent.reshape(64, 128))


def assemble_kernel(*refs):
    out_ref, token_ref = refs[-2:]
    size = refs[0].shape[0]
    for k, ref in enumerate(refs[:4]):
        at = pl.multiple_of(lax.rem(here("z") + k, 4) * size, size)
        out_ref[pl.ds(at, size), :] = ref[...]
    token_ref[...] = jnp.zeros_like(token_ref)


def assemble(parts, after):
    size = parts[0].shape[0]
    return pl.pallas_call(
        assemble_kernel,
        in_specs=[VMEM] * 4 + [ANY],
        out_specs=[VMEM] * 2,
        out_shape=[
            jax.ShapeDtypeStruct((4 * size, D), bf16),
            jax.ShapeDtypeStruct((8, 128), f32),
        ],
        compiler_params=params(8),
        cost_estimate=cost(0, size * D * 16),
    )(*parts, after)


def row_parts(refs):
    if len(refs) == 2:
        return [(ref, at) for ref in refs for at in (0, PART)]
    return [(ref, 0) for ref in refs]


def exp_kernel(below, far, n_rows, *refs):
    parts = row_parts(refs[:n_rows])
    f0, f1, f2, f3, labels_ref = refs[n_rows : n_rows + 5]
    refs = refs[n_rows + 5 :]
    exp_ref, sums_ref = refs[-2:]
    x, y, core = here("x"), here("y"), here("core")
    line = y * 16 + here("z") * 4
    first = (line + lax.rem(x + 4 - below, 4)) * 2
    second = (line + lax.rem(x + 4 - (4 - below if far else below), 4)) * 2
    numbers = (first + core, second + core, first + 1 - core, second + 1 - core)
    places = [
        pl.ds(pl.multiple_of(lax.rem(y + chunk, 4) * 256, 256), 256) for chunk in range(4)
    ]
    totals = [None] * 8
    at_targets = [None] * 8
    for part, (rows_ref, at_row) in enumerate(parts):
        base = (numbers[part] * CLS_DEV).astype(f32)
        tail = rows_ref[at_row + HALF : at_row + PART, 0:128].astype(f32)
        columns = []
        for b in range(3):
            ids = tail[b : b + 1] * 64.0 + tail[3 + b : 4 + b] + base
            columns.append(jnp.broadcast_to(ids, (128, 128)).T)
        for chunk, faces_ref in enumerate((f0, f1, f2, f3)):
            cosine = lax.dot_general(
                rows_ref[at_row : at_row + HALF, :],
                faces_ref[...],
                (((1,), (1,)), ((), ())),
                preferred_element_type=f32,
            )
            labels = labels_ref[0:1, places[chunk]]
            for half in range(2):
                lane = chunk * 2 + half
                lanes = slice(lane * 128, lane * 128 + 128)
                wanted = labels[:, half * 128 : half * 128 + 128]
                total, at_target = totals[lane], at_targets[lane]
                for b in range(3):
                    cos = cosine[b * 128 : b * 128 + 128, half * 128 : half * 128 + 128]
                    hit = columns[b] == wanted
                    expo = jnp.where(hit, 0.0, jnp.exp2(cos * exp2_scale))
                    at = part * HALF + b * 128
                    exp_ref[at : at + 128, lanes] = expo.astype(bf16)
                    expo = jnp.sum(expo.reshape(16, 8, 128), axis=0)
                    chosen = jnp.sum(jnp.where(hit, cos, 0.0).reshape(16, 8, 128), axis=0)
                    total = expo if total is None else total + expo
                    at_target = chosen if at_target is None else at_target + chosen
                totals[lane], at_targets[lane] = total, at_target
    for chunk in range(4):
        for row, found in ((0, totals), (1, at_targets)):
            both = jnp.concatenate([found[2 * chunk], found[2 * chunk + 1]], axis=1)
            value = jnp.sum(both, axis=0, keepdims=True)
            if below:
                value = value + refs[0][row : row + 1, places[chunk]]
            sums_ref[row : row + 1, places[chunk]] = value


def exp_block(below, rows, faces, labels, *others):
    return pl.pallas_call(
        functools.partial(exp_kernel, below, below == 2, len(rows)),
        in_specs=[VMEM] * (5 + len(rows) + (len(others) if below else 0)) + ([] if below else [ANY] * len(others)),
        out_specs=[VMEM] * 2,
        out_shape=[
            jax.ShapeDtypeStruct((4 * HALF, FACES), bf16),
            jax.ShapeDtypeStruct((2, FACES), f32),
        ],
        compiler_params=params(8),
        cost_estimate=cost(0, 0),
    )(*rows, *faces, labels, *others)


def coefficients(sums_ref, weight_ref):
    others = sums_ref[0:1, :]
    cos_t = sums_ref[1:2, :]
    sine_root = jnp.sqrt(1.001 - cos_t * cos_t)
    logit_t = logit_scale * (cos_t * cos_margin - sine_root * sin_margin)
    scaled = weight_ref[...] / (others + jnp.exp(logit_t))
    slope = logit_scale * (cos_margin + sin_margin * cos_t / sine_root)
    return scaled * logit_scale, -scaled * others * slope


def chunk_places(y):
    return [pl.ds(pl.multiple_of(lax.rem(y + chunk, 4) * 256, 256), 256) for chunk in range(4)]


def sum_kernel(first, n_rows, exp_ref, *refs):
    parts = row_parts(refs[:n_rows])
    refs = refs[n_rows:]
    sum_ref, target_ref, mark_ref = refs[-3:]
    for chunk in range(4):
        lanes = slice(chunk * 256, chunk * 256 + 256)
        summed = None if first else refs[0][:, lanes]
        chosen = None if first else refs[1][:, lanes]
        for part, (rows_ref, at_row) in enumerate(parts):
            expo = exp_ref[part * HALF : part * HALF + HALF, lanes]
            mark_ref[chunk] = jnp.where(expo.astype(f32) == 0.0, 1.0, 0.0).astype(bf16)
            rows = rows_ref[at_row : at_row + HALF, :]
            over_rows = (((0,), (0,)), ((), ()))
            term = lax.dot_general(rows, expo, over_rows, preferred_element_type=f32)
            summed = term if summed is None else summed + term
            term = lax.dot_general(rows, mark_ref[chunk], over_rows, preferred_element_type=f32)
            chosen = term if chosen is None else chosen + term
        sum_ref[:, lanes] = summed
        target_ref[:, lanes] = chosen


def sum_block(expo, rows, before, *after):
    def kernel(*refs):
        n = 1 + len(rows) + len(before)
        sum_kernel(not before, len(rows), *refs[:n], *refs[n + len(after) :])

    return pl.pallas_call(
        kernel,
        in_specs=[VMEM] * (1 + len(rows) + len(before)) + [ANY] * len(after),
        out_specs=[VMEM] * 2,
        out_shape=[jax.ShapeDtypeStruct((D, FACES), f32)] * 2,
        scratch_shapes=[pltpu.VMEM((4, HALF, 256), bf16)],
        compiler_params=params(10),
        cost_estimate=cost(4 * 4 * HALF * FACES * D, 6 * 1024 * 1024),
    )(expo, *rows, *before, *after)


def face_sum_kernel(sum_ref, target_ref, sums_ref, weight_ref, *refs):
    coef_ref = refs[-1]
    coef_ref[0:1, :], coef_ref[1:2, :] = coefficients(sums_ref, weight_ref)
    for chunk, place in enumerate(chunk_places(here("y"))):
        lanes = slice(chunk * 256, chunk * 256 + 256)
        value = sum_ref[:, lanes] * coef_ref[0:1, place] + target_ref[:, lanes] * coef_ref[1:2, place]
        refs[chunk - 5][...] = value.T.astype(bf16)


def face_sums(summed, chosen, sums, weight, *after):
    return pl.pallas_call(
        face_sum_kernel,
        in_specs=[VMEM] * 4 + [ANY] * len(after),
        out_specs=[VMEM] * 4,
        out_shape=[jax.ShapeDtypeStruct((256, D), bf16)] * 4,
        scratch_shapes=[pltpu.VMEM((2, FACES), f32)],
        compiler_params=params(8),
        cost_estimate=cost(0, 0),
    )(summed, chosen, sums, weight, *after)


def grad_kernel(exp_ref, f0, f1, f2, f3, sums_ref, weight_ref, *refs):
    cg_own_ref, cg_mate_ref, coef_ref, dcos_ref = refs[-4:]
    coef_ref[0:1, :], coef_ref[1:2, :] = coefficients(sums_ref, weight_ref)
    places = chunk_places(here("y"))
    coef = [coef_ref[0:1, place] for place in places]
    target_coef = [coef_ref[1:2, place] for place in places]
    for part in (2, 3, 0, 1):
        rows = slice(part * HALF, part * HALF + HALF)
        for chunk in range(4):
            lanes = slice(chunk * 256, chunk * 256 + 256)
            expo = exp_ref[rows, lanes].astype(f32)
            dcos_ref[part, :, lanes] = jnp.where(
                expo == 0.0, target_coef[chunk], expo * coef[chunk]
            ).astype(bf16)
        grad = None
        for chunk, faces_ref in enumerate((f0, f1, f2, f3)):
            lanes = slice(chunk * 256, chunk * 256 + 256)
            term = jnp.dot(dcos_ref[part, :, lanes], faces_ref[...], preferred_element_type=f32)
            grad = term if grad is None else grad + term
        cg_ref = (cg_own_ref, cg_mate_ref)[part // 2]
        cg_ref[(part % 2) * HALF : (part % 2) * HALF + HALF, :] = grad.astype(bf16)


def grad_block(expo, faces, sums, weight, *after):
    return pl.pallas_call(
        grad_kernel,
        in_specs=[VMEM] * 7 + [ANY] * len(after),
        out_specs=[VMEM] * 2,
        out_shape=[jax.ShapeDtypeStruct((SAMPLE, D), bf16)] * 2,
        scratch_shapes=[
            pltpu.VMEM((2, FACES), f32),
            pltpu.VMEM((4, HALF, FACES), bf16),
        ],
        compiler_params=params(10),
        cost_estimate=cost(0, 0),
    )(expo, *faces, sums, weight, *after)


def join_kernel(at, own_ref, mate_ref, *refs):
    out_ref = refs[-1]
    for half in range(2):
        rows = slice(half * HALF, half * HALF + HALF)
        value = own_ref[rows, :].astype(f32) + mate_ref[rows, :].astype(f32)
        if at == half:
            value = value + refs[0][...].astype(f32)
        out_ref[rows, :] = value.astype(bf16)


def join(cg, from_mate, at, arrived, *after):
    return pl.pallas_call(
        functools.partial(join_kernel, at),
        in_specs=[VMEM] * 3 + [ANY] * len(after),
        out_specs=VMEM,
        out_shape=jax.ShapeDtypeStruct((SAMPLE, D), bf16),
        compiler_params=params(8),
        cost_estimate=cost(SAMPLE * D * 2, SAMPLE * D * 6),
    )(cg, from_mate, arrived, *after)


def join_halves_kernel(own_ref, mate_ref, *out_refs):
    for half, out_ref in enumerate(out_refs):
        rows = slice(half * HALF, half * HALF + HALF)
        out_ref[...] = (own_ref[rows, :].astype(f32) + mate_ref[rows, :].astype(f32)).astype(bf16)


def join_halves(cg, from_mate):
    return pl.pallas_call(
        join_halves_kernel,
        in_specs=[VMEM] * 2,
        out_specs=[VMEM] * 2,
        out_shape=[jax.ShapeDtypeStruct((HALF, D), bf16)] * 2,
        compiler_params=params(8),
        cost_estimate=cost(SAMPLE * D * 2, SAMPLE * D * 6),
    )(cg, from_mate)


def rows_base_kernel(picked_ref, mom_ref, own_ref, mate_ref, base_ref):
    picked = picked_ref[...].astype(f32)
    inverse = inverse_norm(picked)
    rows32 = picked * inverse
    grad = own_ref[...].astype(f32) + mate_ref[...].astype(f32)
    row_grad = inverse * (grad - rows32 * jnp.sum(rows32 * grad, axis=1, keepdims=True))
    base_ref[...] = momentum_rate * mom_ref[...].astype(f32) + row_grad


def rows_base(*arrays):
    return pl.pallas_call(
        rows_base_kernel,
        in_specs=[VMEM] * 4,
        out_specs=VMEM,
        out_shape=jax.ShapeDtypeStruct((SAMPLE, D), f32),
        compiler_params=params(8),
        cost_estimate=cost(SAMPLE * D * 20, SAMPLE * D * 16),
    )(*arrays)


def rows_end_kernel(picked_ref, base_ref, v0_ref, v1_ref, velocity_ref, new_ref, velocity_buf, new_buf, sem):
    copies = []
    for half in range(2):
        rows = slice(half * HALF, half * HALF + HALF)
        picked = picked_ref[rows, :].astype(f32)
        inverse = inverse_norm(picked)
        rows32 = picked * inverse
        grad = v0_ref[rows, :].astype(f32) + v1_ref[rows, :].astype(f32)
        row_grad = inverse * (grad - rows32 * jnp.sum(rows32 * grad, axis=1, keepdims=True))
        velocity = base_ref[rows, :] + row_grad
        velocity_buf[rows, :] = velocity
        new_buf[rows, :] = (picked - learn_rate * velocity).astype(bf16)
        place = pl.ds(half * HALF, HALF)
        for i, (buf, ref) in enumerate(((velocity_buf, velocity_ref), (new_buf, new_ref))):
            copy = pltpu.make_async_copy(buf.at[place, :], ref.at[place, :], sem.at[half, i])
            copy.start()
            copies.append(copy)
    for copy in copies:
        copy.wait()


def rows_end(*arrays):
    return pl.pallas_call(
        rows_end_kernel,
        in_specs=[VMEM] * 4,
        out_specs=[HBM] * 2,
        out_shape=[
            jax.ShapeDtypeStruct((SAMPLE, D), f32),
            jax.ShapeDtypeStruct((SAMPLE, D), bf16),
        ],
        scratch_shapes=[
            pltpu.VMEM((SAMPLE, D), f32),
            pltpu.VMEM((SAMPLE, D), bf16),
            pltpu.SemaphoreType.DMA((2, 2)),
        ],
        compiler_params=params(8),
        cost_estimate=cost(SAMPLE * D * 20, SAMPLE * D * 16),
    )(*arrays)


def split_kernel(a_ref, b_ref, c_ref, d_ref, *refs):
    for k, out_ref in enumerate(refs[-4:]):
        rows = pl.ds(pl.multiple_of(lax.rem(here("z") + k, 4) * 64, 64), 64)
        out_ref[...] = (
            a_ref[rows, :].astype(f32)
            + b_ref[rows, :].astype(f32)
            + c_ref[rows, :].astype(f32)
            + d_ref[rows, :].astype(f32)
        ).astype(bf16)


def split(parts, *after):
    return pl.pallas_call(
        split_kernel,
        in_specs=[VMEM] * 4 + [ANY] * len(after),
        out_specs=[VMEM] * 4,
        out_shape=[jax.ShapeDtypeStruct((64, D), bf16)] * 4,
        compiler_params=params(8),
        cost_estimate=cost(256 * D * 4, 256 * D * 10),
    )(*parts, *after)


def faces_end_kernel(emb_ref, sums_ref, a_ref, b_ref, c_ref, d_ref, *refs):
    out_ref, loss_ref = refs[-2:]
    start = pl.multiple_of(here("core") * 64, 64)
    values = emb_ref[pl.ds(start, 64), :].astype(f32)
    inverse = inverse_norm(values)
    unit = values * inverse
    summed = (
        a_ref[...].astype(f32)
        + b_ref[...].astype(f32)
        + c_ref[...].astype(f32)
        + d_ref[...].astype(f32)
    )
    out_ref[...] = inverse * (summed - unit * jnp.sum(unit * summed, axis=1, keepdims=True))
    block = here("y") * 4 + here("z")
    lanes = pl.ds(pl.multiple_of(lax.div(block, 2) * 128, 128), 128)
    cos_t = sums_ref[1:2, lanes]
    sine_root = jnp.sqrt(1.001 - cos_t * cos_t)
    logit_t = logit_scale * (cos_t * cos_margin - sine_root * sin_margin)
    loss = jnp.log(sums_ref[0:1, lanes] + jnp.exp(logit_t)) - logit_t
    loss_ref[...] = jnp.where(lax.rem(block, 2) == 0, loss, pltpu.roll(loss, 64, 1))


def faces_end(embeddings, sums, parts, *after):
    return pl.pallas_call(
        faces_end_kernel,
        in_specs=[VMEM] * 6 + [ANY] * len(after),
        out_specs=[VMEM] * 2,
        out_shape=[
            jax.ShapeDtypeStruct((64, D), f32),
            jax.ShapeDtypeStruct((1, 128), f32),
        ],
        compiler_params=params(8),
        cost_estimate=cost(64 * D * 12, 64 * D * 16),
    )(embeddings, sums, *parts, *after)


def both_cores_kernel(grad_ref, mate_grad_ref, loss_ref, mate_loss_ref, out_ref, out_loss_ref):
    core = here("core")
    out_ref[pl.ds(pl.multiple_of(core * 64, 64), 64), :] = grad_ref[...]
    out_ref[pl.ds(pl.multiple_of(64 - core * 64, 64), 64), :] = mate_grad_ref[...]
    lane = lax.broadcasted_iota(jnp.int32, (1, 128), 1)
    low = jnp.where(core == 0, loss_ref[...], mate_loss_ref[...])
    high = jnp.where(core == 0, mate_loss_ref[...], loss_ref[...])
    out_loss_ref[...] = jnp.where(lane < 64, low, pltpu.roll(high, 64, 1))


def both_cores(*arrays):
    return pl.pallas_call(
        both_cores_kernel,
        in_specs=[VMEM] * 4,
        out_specs=[VMEM] * 2,
        out_shape=[
            jax.ShapeDtypeStruct((128, D), f32),
            jax.ShapeDtypeStruct((1, 128), f32),
        ],
        compiler_params=params(8),
        cost_estimate=cost(0, 64 * D * 16),
    )(*arrays)


def shift(array, axis, k):
    return lax.ppermute(array, axis, [((i + k) % 4, i) for i in range(4)])


def swap(array):
    return lax.ppermute(array, "core", [(0, 1), (1, 0)])


def total(array, axis):
    return array + shift(array, axis, 2) + shift(array, axis, 1) + shift(array, axis, 3)


def gather_rows(array, ids):
    return lax.gather(
        array,
        ids[:, None],
        lax.GatherDimensionNumbers(
            offset_dims=(1,), collapsed_slice_dims=(0,), start_index_map=(0,)
        ),
        slice_sizes=(1, D),
        mode=lax.GatherScatterMode.PROMISE_IN_BOUNDS,
    )


def shards(embeddings, labels, centres, momentum, sample_rows, cotangent):
    picked = gather_rows(centres, sample_rows)
    message, unit, my_labels, weight = prepare(
        picked, sample_rows, embeddings, labels, cotangent
    )

    up = shift(message, "x", -1)
    down = shift(message, "x", 1)
    own_rows = [message, swap(message)]

    plane, token = assemble(
        [unit] + [shift(unit, "z", k) for k in (1, 2, 3)], own_rows[1]
    )
    faces = [plane] + [shift(plane, "y", k) for k in (1, 2, 3)]

    up, down = tie(up, *faces[1:]), tie(down, *faces[1:])
    c0, d1 = cut(0, up), cut(1, down)
    up, down = tie(up, c0, d1), tie(down, c0, d1)
    c0, d1 = shift(c0, "x", -1), shift(d1, "x", 1)

    expo = {}
    expo["own"], sums_own = exp_block(0, own_rows, faces, my_labels)
    up_rows = [up, swap(up)]
    expo["up"], sums_up = exp_block(1, up_rows, faces, my_labels, sums_own)
    face_sum = sum_block(expo["own"], own_rows, (), sums_up)
    down_rows = [down, swap(down)]
    expo["down"], sums_down = exp_block(3, down_rows, faces, my_labels, sums_up)
    c0, d1 = tie(c0, face_sum[0]), tie(d1, face_sum[0])
    far_rows = [c0, d1, swap(c0), swap(d1)]
    expo["far"], sums = exp_block(2, far_rows, faces, my_labels, sums_down)
    face_sum = sum_block(expo["up"], up_rows, face_sum, sums)
    sums = total(sums, "y")
    face_sum = sum_block(expo["down"], down_rows, face_sum, sums)
    sums = total(sums, "z")
    sums = tie(sums, face_sum[0])

    def grads(name, *after):
        return grad_block(expo[name], faces, sums, weight, *after)

    far_own, far_mate = grads("far")
    up_own, up_mate = grads("up", far_mate)
    down_own, down_mate = grads("down", up_mate)
    far_mate, up_mate, down_mate = swap(far_mate), swap(up_mate), swap(down_mate)
    face_sum = sum_block(expo["far"], far_rows, face_sum, down_own)
    t0, t1 = join_halves(far_own, far_mate)
    r0, r1 = shift(t0, "x", 1), shift(t1, "x", -1)
    parts = face_sums(*face_sum, sums, weight, t0, up_mate, down_mate)
    cg_own, cg_mate = grads("own", parts[0])
    v_up = join(up_own, up_mate, 0, r0)
    v_down = join(down_own, down_mate, 1, r1)
    v0, v1 = shift(v_up, "x", 1), shift(v_down, "x", -1)

    mom_rows = gather_rows(momentum, tie(sample_rows, v_up, v_down, cg_own))
    parts = split(
        [parts[0]] + [shift(parts[k], "y", -k) for k in (1, 2, 3)], v_up, v_down, mom_rows
    )
    parts = [parts[0]] + [shift(parts[k], "z", -k) for k in (1, 2, 3)]
    base = rows_base(picked, mom_rows, cg_own, swap(tie(cg_mate, parts[0])))
    half_grad, half_loss = faces_end(embeddings, sums, parts, v0, v1)
    grad_embed, loss = both_cores(half_grad, swap(half_grad), half_loss, swap(half_loss))

    velocity, new_rows = rows_end(picked, base, v0, v1)
    return (loss.reshape(128), grad_embed, velocity, new_rows)


def solution(mesh):
    grid = Mesh(mesh.devices.reshape(4, 4, 4, 2), ("y", "z", "x", "core"))
    chips = ("y", "z", "x")
    devices = ("y", "z", "x", "core")
    return jax.shard_map(
        shards,
        mesh=grid,
        in_specs=(
            P(chips, None),
            P(),
            P(devices, None),
            P(devices, None),
            P(devices),
            P(),
        ),
        out_specs=(P(chips), P(chips, None), P(devices, None), P(devices, None)),
        check_vma=False,
    )
```

```python
import functools

import jax
import jax.numpy as jnp
from jax import lax
from jax.experimental import pallas as pl
from jax.experimental.pallas import tpu as pltpu
from jax.sharding import Mesh
from jax.sharding import PartitionSpec as P

logit_scale = 64.0
cos_margin = 0.8775825618903728
sin_margin = 0.479425538604203
momentum_rate = 0.9
learn_rate = 0.1
exp2_scale = 64.0 * 1.4426950408889634

D = 512
SAMPLE = 768
TAIL = 16
HALF = SAMPLE // 2
MSG = SAMPLE + TAIL
FACES = 1024
CLS_DEV = 8192
bf16 = jnp.bfloat16
f32 = jnp.float32
VMEM = pl.BlockSpec(memory_space=pltpu.VMEM)
HBM = pl.BlockSpec(memory_space=pltpu.HBM)
ANY = pl.BlockSpec(memory_space=pl.ANY)
SMEM = pl.BlockSpec(memory_space=pltpu.SMEM)


def params(mib):
    return pltpu.CompilerParams(vmem_limit_bytes=mib * 1024 * 1024)


def cost(flops, bytes_accessed, transcendentals=0):
    return pl.CostEstimate(
        flops=flops // 16, bytes_accessed=bytes_accessed // 16, transcendentals=transcendentals // 16
    )


def inverse_norm(values):
    return lax.rsqrt(jnp.sum(values * values, axis=1, keepdims=True) + 1e-06)


def here(axis):
    return lax.axis_index(axis).astype(jnp.int32)


def tie(array, *others):
    def nothing(*refs):
        pass

    return pl.pallas_call(
        nothing,
        in_specs=[ANY] * (1 + len(others)),
        out_specs=ANY,
        out_shape=jax.ShapeDtypeStruct(array.shape, array.dtype),
        input_output_aliases={0: 0},
        compiler_params=params(1),
    )(array, *others)


def copy_kernel(array_ref, *refs):
    refs[-1][...] = array_ref[...]


def copied(array, *others):
    return pl.pallas_call(
        copy_kernel,
        in_specs=[VMEM] + [ANY] * len(others),
        out_specs=VMEM,
        out_shape=jax.ShapeDtypeStruct(array.shape, array.dtype),
        compiler_params=params(1),
    )(array, *others)


def my_faces(table_ref, out_ref):
    x, core = here("x"), here("core")
    lane = lax.broadcasted_iota(jnp.int32, (1, 128), 1)
    for pair in range(8):
        left = table_ref[pl.ds(pair * 8 + x, 1), :].astype(f32)
        right = table_ref[pl.ds(pair * 8 + 4 + x, 1), :].astype(f32)
        left = jnp.where(core == 0, left, pltpu.roll(left, 64, 1))
        right = jnp.where(core == 0, pltpu.roll(right, 64, 1), right)
        out_ref[:, pair * 128 : pair * 128 + 128] = jnp.where(lane < 64, left, right)


def prepare_kernel(picked_ref, ids_ref, emb_ref, labels_ref, weight_ref, out_ref, unit_ref, my_labels_ref, my_weight_ref, tail_ref):
    start = pl.multiple_of(here("core") * 64, 64)
    values = emb_ref[pl.ds(start, 64), :].astype(f32)
    unit_ref[...] = (values * inverse_norm(values)).astype(bf16)
    ids = ids_ref[...]
    high = (ids >> 6).astype(f32)
    low = (ids & 63).astype(f32)
    values = picked_ref[...].astype(f32)
    out_ref[0:SAMPLE, :] = (values * inverse_norm(values)).astype(bf16)
    tail_ref[...] = jnp.zeros_like(tail_ref)
    tail_ref[0:6, 0:128] = high
    tail_ref[6:12, 0:128] = low
    out_ref[SAMPLE:MSG, :] = tail_ref[...].astype(bf16)
    my_faces(labels_ref, my_labels_ref)
    my_faces(weight_ref, my_weight_ref)


def cut_kernel(first, array_ref, out_ref):
    out_ref[...] = array_ref[first : first + out_ref.shape[0], :]


def cut(message, first, size):
    return pl.pallas_call(
        functools.partial(cut_kernel, first),
        in_specs=[VMEM],
        out_specs=VMEM,
        out_shape=jax.ShapeDtypeStruct((size, D), bf16),
        compiler_params=params(2),
        cost_estimate=cost(0, 0),
    )(message)


def paste_kernel(top_ref, bottom_ref, *refs):
    refs[-1][0:HALF, :] = top_ref[...]
    refs[-1][HALF:MSG, :] = bottom_ref[...]


def paste(top, bottom, *after):
    return pl.pallas_call(
        paste_kernel,
        in_specs=[VMEM] * 2 + [ANY] * len(after),
        out_specs=VMEM,
        out_shape=jax.ShapeDtypeStruct((MSG, D), bf16),
        compiler_params=params(4),
        cost_estimate=cost(0, 0),
    )(top, bottom, *after)


def prepare(picked, ids, embeddings, labels, cotangent):
    return pl.pallas_call(
        prepare_kernel,
        in_specs=[VMEM] * 5,
        out_specs=[VMEM] * 4,
        out_shape=[
            jax.ShapeDtypeStruct((MSG, D), bf16),
            jax.ShapeDtypeStruct((64, D), bf16),
            jax.ShapeDtypeStruct((1, FACES), f32),
            jax.ShapeDtypeStruct((1, FACES), f32),
        ],
        scratch_shapes=[pltpu.VMEM((TAIL, D), f32)],
        compiler_params=params(8),
        cost_estimate=cost(SAMPLE * D * 4, SAMPLE * D * 4),
    )(picked, ids.reshape(6, 128), embeddings, labels.reshape(64, 128), cotangent.reshape(64, 128))


def assemble_kernel(*refs):
    out_ref, token_ref = refs[-2:]
    size = refs[0].shape[0]
    for k, ref in enumerate(refs[:4]):
        at = pl.multiple_of(lax.rem(here("z") + k, 4) * size, size)
        out_ref[pl.ds(at, size), :] = ref[...]
    token_ref[...] = jnp.zeros_like(token_ref)


def assemble(parts, after):
    size = parts[0].shape[0]
    return pl.pallas_call(
        assemble_kernel,
        in_specs=[VMEM] * 4 + [ANY],
        out_specs=[VMEM] * 2,
        out_shape=[
            jax.ShapeDtypeStruct((4 * size, D), bf16),
            jax.ShapeDtypeStruct((8, 128), f32),
        ],
        compiler_params=params(8),
        cost_estimate=cost(0, size * D * 16),
    )(*parts, after)


def chunk_places(y):
    return [pl.ds(pl.multiple_of(lax.rem(y + chunk, 4) * 256, 256), 256) for chunk in range(4)]


def exp_kernel(away, own_ref, mate_ref, f0, f1, f2, f3, labels_ref, *refs):
    exp_ref, sums_ref = refs[-2:]
    core = here("core")
    first = (here("y") * 16 + here("z") * 4 + lax.rem(here("x") + away, 4)) * 2
    places = chunk_places(here("y"))
    totals = [None] * 8
    at_targets = [None] * 8
    for part, (rows_ref, shard) in enumerate(((own_ref, first + core), (mate_ref, first + 1 - core))):
        base = (shard * CLS_DEV).astype(f32)
        tail = rows_ref[SAMPLE:MSG, 0:128].astype(f32)
        columns = []
        for b in range(6):
            ids = tail[b : b + 1] * 64.0 + tail[6 + b : 7 + b] + base
            columns.append(jnp.broadcast_to(ids, (128, 128)).T)
        for quarter in range(8):
            row, chunk = (quarter // 4) * HALF, quarter % 4
            cosine = lax.dot_general(
                rows_ref[row : row + HALF, :],
                (f0, f1, f2, f3)[chunk][...],
                (((1,), (1,)), ((), ())),
                preferred_element_type=f32,
            )
            labels = labels_ref[0:1, places[chunk]]
            for half in range(2):
                lane = chunk * 2 + half
                lanes = slice(lane * 128, lane * 128 + 128)
                wanted = labels[:, half * 128 : half * 128 + 128]
                total, at_target = totals[lane], at_targets[lane]
                for b in range(3):
                    cos = cosine[b * 128 : b * 128 + 128, half * 128 : half * 128 + 128]
                    hit = columns[row // 128 + b] == wanted
                    expo = jnp.where(hit, 0.0, jnp.exp2(cos * exp2_scale))
                    at = part * SAMPLE + row + b * 128
                    exp_ref[at : at + 128, lanes] = expo.astype(bf16)
                    expo = jnp.sum(expo.reshape(16, 8, 128), axis=0)
                    chosen = jnp.sum(jnp.where(hit, cos, 0.0).reshape(16, 8, 128), axis=0)
                    total = expo if total is None else total + expo
                    at_target = chosen if at_target is None else at_target + chosen
                totals[lane], at_targets[lane] = total, at_target
    for chunk in range(4):
        for row, found in ((0, totals), (1, at_targets)):
            both = jnp.concatenate([found[2 * chunk], found[2 * chunk + 1]], axis=1)
            value = jnp.sum(both, axis=0, keepdims=True)
            if away:
                value = value + refs[0][row : row + 1, places[chunk]]
            sums_ref[row : row + 1, places[chunk]] = value


def exp_block(away, rows, faces, labels, *before):
    return pl.pallas_call(
        functools.partial(exp_kernel, away),
        in_specs=[VMEM] * (7 + len(before)),
        out_specs=[VMEM] * 2,
        out_shape=[
            jax.ShapeDtypeStruct((2 * SAMPLE, FACES), bf16),
            jax.ShapeDtypeStruct((2, FACES), f32),
        ],
        compiler_params=params(8),
        cost_estimate=cost(0, 0),
    )(*rows, *faces, labels, *before)


def coefficients(sums_ref, weight_ref):
    others = sums_ref[0:1, :]
    cos_t = sums_ref[1:2, :]
    sine_root = jnp.sqrt(1.001 - cos_t * cos_t)
    logit_t = logit_scale * (cos_t * cos_margin - sine_root * sin_margin)
    scaled = weight_ref[...] / (others + jnp.exp(logit_t))
    slope = logit_scale * (cos_margin + sin_margin * cos_t / sine_root)
    return scaled * logit_scale, -scaled * others * slope


def sum_kernel(exp_ref, own_ref, mate_ref, *refs):
    sum_ref, target_ref, mark_ref = refs[-3:]
    over_rows = (((0,), (0,)), ((), ()))
    for chunk in range(2):
        lanes = slice(chunk * 512, chunk * 512 + 512)
        summed, chosen = (ref[:, lanes] for ref in refs[:2]) if len(refs) > 3 else (None, None)
        for part, rows_ref in enumerate((own_ref, mate_ref)):
            expo = exp_ref[part * SAMPLE : part * SAMPLE + SAMPLE, lanes]
            mark_ref[part] = jnp.where(expo.astype(f32) == 0.0, 1.0, 0.0).astype(bf16)
            rows = rows_ref[0:SAMPLE, :]
            term = lax.dot_general(rows, expo, over_rows, preferred_element_type=f32)
            summed = term if summed is None else summed + term
            term = lax.dot_general(rows, mark_ref[part], over_rows, preferred_element_type=f32)
            chosen = term if chosen is None else chosen + term
        sum_ref[:, lanes] = summed
        target_ref[:, lanes] = chosen


def sum_block(expo, rows, before, *after):
    def kernel(*refs):
        n = 3 + len(before)
        sum_kernel(*refs[:n], *refs[n + len(after) :])

    return pl.pallas_call(
        kernel,
        in_specs=[VMEM] * (3 + len(before)) + [ANY] * len(after),
        out_specs=[VMEM] * 2,
        out_shape=[jax.ShapeDtypeStruct((D, FACES), f32)] * 2,
        scratch_shapes=[pltpu.VMEM((2, SAMPLE, 512), bf16)],
        compiler_params=params(12),
        cost_estimate=cost(4 * 4 * HALF * FACES * D, 6 * 1024 * 1024),
    )(expo, *rows, *before, *after)


def face_sum_kernel(sum_ref, target_ref, sums_ref, weight_ref, *refs):
    coef_ref = refs[-1]
    coef_ref[0:1, :], coef_ref[1:2, :] = coefficients(sums_ref, weight_ref)
    for chunk, place in enumerate(chunk_places(here("y"))):
        lanes = slice(chunk * 256, chunk * 256 + 256)
        value = sum_ref[:, lanes] * coef_ref[0:1, place] + target_ref[:, lanes] * coef_ref[1:2, place]
        refs[chunk - 5][...] = value.T.astype(bf16)


def face_sums(summed, chosen, sums, weight, *after):
    return pl.pallas_call(
        face_sum_kernel,
        in_specs=[VMEM] * 4 + [ANY] * len(after),
        out_specs=[VMEM] * 4,
        out_shape=[jax.ShapeDtypeStruct((256, D), bf16)] * 4,
        scratch_shapes=[pltpu.VMEM((2, FACES), f32)],
        compiler_params=params(8),
        cost_estimate=cost(0, 0),
    )(summed, chosen, sums, weight, *after)


def grad_kernel(exp_ref, f0, f1, f2, f3, sums_ref, weight_ref, *refs):
    cg_own_ref, cg_mate_ref, coef_ref, dcos_ref = refs[-4:]
    coef_ref[0:1, :], coef_ref[1:2, :] = coefficients(sums_ref, weight_ref)
    places = chunk_places(here("y"))
    coef = [coef_ref[0:1, place] for place in places]
    target_coef = [coef_ref[1:2, place] for place in places]
    for part, cg_ref in ((1, cg_mate_ref), (0, cg_own_ref)):
        rows = slice(part * SAMPLE, part * SAMPLE + SAMPLE)
        for chunk in range(4):
            lanes = slice(chunk * 256, chunk * 256 + 256)
            expo = exp_ref[rows, lanes].astype(f32)
            dcos_ref[part, :, lanes] = jnp.where(
                expo == 0.0, target_coef[chunk], expo * coef[chunk]
            ).astype(bf16)
        grad = None
        for chunk, faces_ref in enumerate((f0, f1, f2, f3)):
            lanes = slice(chunk * 256, chunk * 256 + 256)
            term = jnp.dot(dcos_ref[part, :, lanes], faces_ref[...], preferred_element_type=f32)
            grad = term if grad is None else grad + term
        cg_ref[...] = grad.astype(bf16)


def grad_block(expo, faces, sums, weight, *after):
    return pl.pallas_call(
        grad_kernel,
        in_specs=[VMEM] * 7 + [ANY] * len(after),
        out_specs=[VMEM] * 2,
        out_shape=[jax.ShapeDtypeStruct((SAMPLE, D), bf16)] * 2,
        scratch_shapes=[
            pltpu.VMEM((2, FACES), f32),
            pltpu.VMEM((2, SAMPLE, FACES), bf16),
        ],
        compiler_params=params(10),
        cost_estimate=cost(0, 0),
    )(expo, *faces, sums, weight, *after)


def join_kernel(at, own_ref, mate_ref, *refs):
    out_ref = refs[-1]
    for half in range(2):
        rows = slice(half * HALF, half * HALF + HALF)
        value = own_ref[rows, :].astype(f32) + mate_ref[rows, :].astype(f32)
        if at == half:
            value = value + refs[0][...].astype(f32)
        out_ref[rows, :] = value.astype(bf16)


def join(cg, from_mate, at, arrived, *after):
    return pl.pallas_call(
        functools.partial(join_kernel, at),
        in_specs=[VMEM] * 3 + [ANY] * len(after),
        out_specs=VMEM,
        out_shape=jax.ShapeDtypeStruct((SAMPLE, D), bf16),
        compiler_params=params(8),
        cost_estimate=cost(SAMPLE * D * 2, SAMPLE * D * 6),
    )(cg, from_mate, arrived, *after)


def join_halves_kernel(own_ref, mate_ref, *out_refs):
    for half, out_ref in enumerate(out_refs):
        rows = slice(half * HALF, half * HALF + HALF)
        out_ref[...] = (own_ref[rows, :].astype(f32) + mate_ref[rows, :].astype(f32)).astype(bf16)


def join_halves(cg, from_mate):
    return pl.pallas_call(
        join_halves_kernel,
        in_specs=[VMEM] * 2,
        out_specs=[VMEM] * 2,
        out_shape=[jax.ShapeDtypeStruct((HALF, D), bf16)] * 2,
        compiler_params=params(8),
        cost_estimate=cost(SAMPLE * D * 2, SAMPLE * D * 6),
    )(cg, from_mate)


def rows_base_kernel(picked_ref, mom_ref, own_ref, mate_ref, base_ref):
    picked = picked_ref[...].astype(f32)
    inverse = inverse_norm(picked)
    rows32 = picked * inverse
    grad = own_ref[...].astype(f32) + mate_ref[...].astype(f32)
    row_grad = inverse * (grad - rows32 * jnp.sum(rows32 * grad, axis=1, keepdims=True))
    base_ref[...] = momentum_rate * mom_ref[...].astype(f32) + row_grad


def rows_base(*arrays):
    return pl.pallas_call(
        rows_base_kernel,
        in_specs=[VMEM] * 4,
        out_specs=VMEM,
        out_shape=jax.ShapeDtypeStruct((SAMPLE, D), f32),
        compiler_params=params(8),
        cost_estimate=cost(SAMPLE * D * 20, SAMPLE * D * 16),
    )(*arrays)


def rows_end_kernel(picked_ref, base_ref, v0_ref, v1_ref, velocity_ref, new_ref, velocity_buf, new_buf, sem):
    copies = []
    for piece in range(4):
        rows = slice(piece * 192, piece * 192 + 192)
        picked = picked_ref[rows, :].astype(f32)
        inverse = inverse_norm(picked)
        rows32 = picked * inverse
        grad = v0_ref[rows, :].astype(f32) + v1_ref[rows, :].astype(f32)
        row_grad = inverse * (grad - rows32 * jnp.sum(rows32 * grad, axis=1, keepdims=True))
        velocity = base_ref[rows, :] + row_grad
        velocity_buf[rows, :] = velocity
        new_buf[rows, :] = (picked - learn_rate * velocity).astype(bf16)
        place = pl.ds(piece * 192, 192)
        for i, (buf, ref) in enumerate(((velocity_buf, velocity_ref), (new_buf, new_ref))):
            copy = pltpu.make_async_copy(buf.at[place, :], ref.at[place, :], sem.at[piece, i])
            copy.start()
            copies.append(copy)
    for copy in copies:
        copy.wait()


def rows_end(*arrays):
    return pl.pallas_call(
        rows_end_kernel,
        in_specs=[VMEM] * 4,
        out_specs=[HBM] * 2,
        out_shape=[
            jax.ShapeDtypeStruct((SAMPLE, D), f32),
            jax.ShapeDtypeStruct((SAMPLE, D), bf16),
        ],
        scratch_shapes=[
            pltpu.VMEM((SAMPLE, D), f32),
            pltpu.VMEM((SAMPLE, D), bf16),
            pltpu.SemaphoreType.DMA((4, 2)),
        ],
        compiler_params=params(8),
        cost_estimate=cost(SAMPLE * D * 20, SAMPLE * D * 16),
    )(*arrays)


def split_kernel(a_ref, b_ref, c_ref, d_ref, *refs):
    for k, out_ref in enumerate(refs[-4:]):
        rows = pl.ds(pl.multiple_of(lax.rem(here("z") + k, 4) * 64, 64), 64)
        out_ref[...] = (
            a_ref[rows, :].astype(f32)
            + b_ref[rows, :].astype(f32)
            + c_ref[rows, :].astype(f32)
            + d_ref[rows, :].astype(f32)
        ).astype(bf16)


def split(parts, *after):
    return pl.pallas_call(
        split_kernel,
        in_specs=[VMEM] * 4 + [ANY] * len(after),
        out_specs=[VMEM] * 4,
        out_shape=[jax.ShapeDtypeStruct((64, D), bf16)] * 4,
        compiler_params=params(8),
        cost_estimate=cost(256 * D * 4, 256 * D * 10),
    )(*parts, *after)


def faces_end_kernel(emb_ref, sums_ref, a_ref, b_ref, c_ref, d_ref, *refs):
    out_ref = refs[-1]
    start = pl.multiple_of(here("core") * 64, 64)
    values = emb_ref[pl.ds(start, 64), :].astype(f32)
    inverse = inverse_norm(values)
    unit = values * inverse
    summed = (
        a_ref[...].astype(f32)
        + b_ref[...].astype(f32)
        + c_ref[...].astype(f32)
        + d_ref[...].astype(f32)
    )
    out_ref[0:64, :] = inverse * (summed - unit * jnp.sum(unit * summed, axis=1, keepdims=True))
    block = here("y") * 4 + here("z")
    lanes = pl.ds(pl.multiple_of(lax.div(block, 2) * 128, 128), 128)
    cos_t = sums_ref[1:2, lanes]
    sine_root = jnp.sqrt(1.001 - cos_t * cos_t)
    logit_t = logit_scale * (cos_t * cos_margin - sine_root * sin_margin)
    loss = jnp.log(sums_ref[0:1, lanes] + jnp.exp(logit_t)) - logit_t
    loss = jnp.where(lax.rem(block, 2) == 0, loss, pltpu.roll(loss, 64, 1))
    out_ref[64:72, :] = jnp.broadcast_to(jnp.concatenate([loss] * 4, axis=1), (8, D))


def faces_end(embeddings, sums, parts, *after):
    return pl.pallas_call(
        faces_end_kernel,
        in_specs=[VMEM] * 6 + [ANY] * len(after),
        out_specs=VMEM,
        out_shape=jax.ShapeDtypeStruct((72, D), f32),
        compiler_params=params(8),
        cost_estimate=cost(64 * D * 12, 64 * D * 16),
    )(embeddings, sums, *parts, *after)


def both_cores_kernel(half_ref, mate_ref, out_ref, loss_ref):
    core = here("core")
    out_ref[pl.ds(pl.multiple_of(core * 64, 64), 64), :] = half_ref[0:64, :]
    out_ref[pl.ds(pl.multiple_of(64 - core * 64, 64), 64), :] = mate_ref[0:64, :]
    lane = lax.broadcasted_iota(jnp.int32, (1, 128), 1)
    own, mate = half_ref[64:65, 0:128], mate_ref[64:65, 0:128]
    low = jnp.where(core == 0, own, mate)
    high = jnp.where(core == 0, mate, own)
    loss_ref[...] = jnp.where(lane < 64, low, pltpu.roll(high, 64, 1))


def both_cores(*arrays):
    return pl.pallas_call(
        both_cores_kernel,
        in_specs=[VMEM] * 2,
        out_specs=[VMEM] * 2,
        out_shape=[
            jax.ShapeDtypeStruct((128, D), f32),
            jax.ShapeDtypeStruct((1, 128), f32),
        ],
        compiler_params=params(8),
        cost_estimate=cost(0, 64 * D * 16),
    )(*arrays)


def shift(array, axis, k):
    return lax.ppermute(array, axis, [((i + k) % 4, i) for i in range(4)])


def swap(array):
    return lax.ppermute(array, "core", [(0, 1), (1, 0)])


def total(array, axis):
    return array + shift(array, axis, 2) + shift(array, axis, 1) + shift(array, axis, 3)


def gather_rows(array, ids):
    return lax.gather(
        array,
        ids[:, None],
        lax.GatherDimensionNumbers(
            offset_dims=(1,), collapsed_slice_dims=(0,), start_index_map=(0,)
        ),
        slice_sizes=(1, D),
        mode=lax.GatherScatterMode.PROMISE_IN_BOUNDS,
    )


def shards(embeddings, labels, centres, momentum, sample_rows, cotangent):
    picked = gather_rows(centres, sample_rows)
    message, unit, my_labels, weight = prepare(
        picked, sample_rows, embeddings, labels, cotangent
    )

    up = shift(message, "x", -1)
    down = shift(message, "x", 1)
    own_rows = [message, swap(message)]

    plane, token = assemble(
        [unit] + [shift(unit, "z", k) for k in (1, 2, 3)], own_rows[1]
    )
    faces = [plane] + [shift(plane, "y", k) for k in (1, 2, 3)]

    up, down = tie(up, *faces[1:]), tie(down, *faces[1:])
    c0, d1 = cut(up, 0, HALF), cut(down, HALF, MSG - HALF)
    up, down = tie(up, c0, d1), tie(down, c0, d1)
    c0, d1 = shift(c0, "x", -1), shift(d1, "x", 1)

    expo = {}
    expo["own"], sums_own = exp_block(0, own_rows, faces, my_labels)
    up_rows = [up, swap(up)]
    expo["up"], sums_up = exp_block(3, up_rows, faces, my_labels, sums_own)
    face_sum = sum_block(expo["own"], own_rows, (), sums_up)
    down_rows = [down, swap(down)]
    expo["down"], sums_down = exp_block(1, down_rows, faces, my_labels, sums_up)
    far = paste(c0, d1, face_sum[0])
    far_rows = [far, swap(far)]
    expo["far"], sums = exp_block(2, far_rows, faces, my_labels, sums_down)
    face_sum = sum_block(expo["up"], up_rows, face_sum, sums)
    sums = total(sums, "y")
    face_sum = sum_block(expo["down"], down_rows, face_sum, sums)
    sums = total(sums, "z")
    sums = tie(sums, face_sum[0])

    def grads(name, *after):
        return grad_block(expo[name], faces, sums, weight, *after)

    far_own, far_mate = grads("far")
    up_own, up_mate = grads("up", far_mate)
    far_mate, up_mate = swap(far_mate), swap(up_mate)
    t0, t1 = join_halves(far_own, far_mate)
    r0, r1 = shift(t0, "x", 1), shift(t1, "x", -1)
    down_own, down_mate = grads("down", t0)
    down_mate = swap(down_mate)
    face_sum = sum_block(expo["far"], far_rows, face_sum, down_own)
    parts = face_sums(*face_sum, sums, weight, up_mate, down_mate)
    cg_own, cg_mate = grads("own", parts[0])
    v_up = join(up_own, up_mate, 0, r0, cg_own)
    v_down = join(down_own, down_mate, 1, r1, cg_own)
    v0, v1 = shift(v_up, "x", 1), shift(v_down, "x", -1)

    mom_rows = gather_rows(momentum, copied(sample_rows, v_up, v_down))
    parts = split(
        [parts[0]] + [shift(parts[k], "y", -k) for k in (1, 2, 3)], v_up, v_down, mom_rows
    )
    cg_mate = swap(tie(cg_mate, parts[0]))
    parts = [parts[0]] + [shift(parts[k], "z", -k) for k in (1, 2, 3)]
    base = rows_base(picked, mom_rows, cg_own, cg_mate)
    half = faces_end(embeddings, sums, parts, v0, v1)
    grad_embed, loss = both_cores(half, swap(half))

    velocity, new_rows = rows_end(picked, base, v0, v1)
    return (loss.reshape(128), grad_embed, velocity, new_rows)


def solution(mesh):
    grid = Mesh(mesh.devices.reshape(4, 4, 4, 2), ("y", "z", "x", "core"))
    chips = ("y", "z", "x")
    devices = ("y", "z", "x", "core")
    return jax.shard_map(
        shards,
        mesh=grid,
        in_specs=(
            P(chips, None),
            P(),
            P(devices, None),
            P(devices, None),
            P(devices),
            P(),
        ),
        out_specs=(P(chips), P(chips, None), P(devices, None), P(devices, None)),
        check_vma=False,
    )
```

```python
import functools

import jax
import jax.numpy as jnp
from jax import lax
from jax.experimental import pallas as pl
from jax.experimental.pallas import tpu as pltpu
from jax.sharding import Mesh
from jax.sharding import PartitionSpec as P

logit_scale = 64.0
cos_margin = 0.8775825618903728
sin_margin = 0.479425538604203
momentum_rate = 0.9
learn_rate = 0.1
exp2_scale = 64.0 * 1.4426950408889634

D = 512
SAMPLE = 768
TAIL = 16
HALF = SAMPLE // 2
MSG = SAMPLE + TAIL
FACES = 1024
CLS_DEV = 8192
bf16 = jnp.bfloat16
f32 = jnp.float32
VMEM = pl.BlockSpec(memory_space=pltpu.VMEM)
HBM = pl.BlockSpec(memory_space=pltpu.HBM)
ANY = pl.BlockSpec(memory_space=pl.ANY)
SMEM = pl.BlockSpec(memory_space=pltpu.SMEM)


def params(mib):
    return pltpu.CompilerParams(vmem_limit_bytes=mib * 1024 * 1024)


def cost(flops, bytes_accessed, transcendentals=0):
    return pl.CostEstimate(
        flops=flops // 16, bytes_accessed=bytes_accessed // 16, transcendentals=transcendentals // 16
    )


def inverse_norm(values):
    return lax.rsqrt(jnp.sum(values * values, axis=1, keepdims=True) + 1e-06)


def here(axis):
    return lax.axis_index(axis).astype(jnp.int32)


def tie(array, *others):
    def nothing(*refs):
        pass

    return pl.pallas_call(
        nothing,
        in_specs=[ANY] * (1 + len(others)),
        out_specs=ANY,
        out_shape=jax.ShapeDtypeStruct(array.shape, array.dtype),
        input_output_aliases={0: 0},
        compiler_params=params(1),
    )(array, *others)


def copy_kernel(array_ref, *refs):
    refs[-1][...] = array_ref[...]


def copied(array, *others):
    return pl.pallas_call(
        copy_kernel,
        in_specs=[VMEM] + [ANY] * len(others),
        out_specs=VMEM,
        out_shape=jax.ShapeDtypeStruct(array.shape, array.dtype),
        compiler_params=params(1),
    )(array, *others)


def my_faces(table_ref, out_ref):
    x, core = here("x"), here("core")
    lane = lax.broadcasted_iota(jnp.int32, (1, 128), 1)
    for pair in range(8):
        left = table_ref[pl.ds(pair * 8 + x, 1), :].astype(f32)
        right = table_ref[pl.ds(pair * 8 + 4 + x, 1), :].astype(f32)
        left = jnp.where(core == 0, left, pltpu.roll(left, 64, 1))
        right = jnp.where(core == 0, pltpu.roll(right, 64, 1), right)
        out_ref[:, pair * 128 : pair * 128 + 128] = jnp.where(lane < 64, left, right)


def prepare_kernel(picked_ref, ids_ref, emb_ref, labels_ref, weight_ref, out_ref, unit_ref, my_labels_ref, my_weight_ref, tail_ref):
    start = pl.multiple_of(here("core") * 64, 64)
    values = emb_ref[pl.ds(start, 64), :].astype(f32)
    unit_ref[...] = (values * inverse_norm(values)).astype(bf16)
    ids = ids_ref[...]
    high = (ids >> 6).astype(f32)
    low = (ids & 63).astype(f32)
    values = picked_ref[...].astype(f32)
    out_ref[0:SAMPLE, :] = (values * inverse_norm(values)).astype(bf16)
    tail_ref[...] = jnp.zeros_like(tail_ref)
    tail_ref[0:6, 0:128] = high
    tail_ref[6:12, 0:128] = low
    out_ref[SAMPLE:MSG, :] = tail_ref[...].astype(bf16)
    my_faces(labels_ref, my_labels_ref)
    my_faces(weight_ref, my_weight_ref)


def cut_kernel(first, array_ref, out_ref):
    out_ref[...] = array_ref[first : first + out_ref.shape[0], :]


def cut(message, first, size):
    return pl.pallas_call(
        functools.partial(cut_kernel, first),
        in_specs=[VMEM],
        out_specs=VMEM,
        out_shape=jax.ShapeDtypeStruct((size, D), bf16),
        compiler_params=params(2),
        cost_estimate=cost(0, 0),
    )(message)


def paste_kernel(top_ref, bottom_ref, *refs):
    size = top_ref.shape[0]
    refs[-1][0:size, :] = top_ref[...]
    refs[-1][size:, :] = bottom_ref[...]


def paste(top, bottom, *after):
    return pl.pallas_call(
        paste_kernel,
        in_specs=[VMEM] * 2 + [ANY] * len(after),
        out_specs=VMEM,
        out_shape=jax.ShapeDtypeStruct((top.shape[0] + bottom.shape[0], D), bf16),
        compiler_params=params(4),
        cost_estimate=cost(0, 0),
    )(top, bottom, *after)


def prepare(picked, ids, embeddings, labels, cotangent):
    return pl.pallas_call(
        prepare_kernel,
        in_specs=[VMEM] * 5,
        out_specs=[VMEM] * 4,
        out_shape=[
            jax.ShapeDtypeStruct((MSG, D), bf16),
            jax.ShapeDtypeStruct((64, D), bf16),
            jax.ShapeDtypeStruct((1, FACES), f32),
            jax.ShapeDtypeStruct((1, FACES), f32),
        ],
        scratch_shapes=[pltpu.VMEM((TAIL, D), f32)],
        compiler_params=params(8),
        cost_estimate=cost(SAMPLE * D * 4, SAMPLE * D * 4),
    )(picked, ids.reshape(6, 128), embeddings, labels.reshape(64, 128), cotangent.reshape(64, 128))


def assemble_kernel(*refs):
    out_ref, token_ref = refs[-2:]
    size = refs[0].shape[0]
    for k, ref in enumerate(refs[:4]):
        at = pl.multiple_of(lax.rem(here("z") + k, 4) * size, size)
        out_ref[pl.ds(at, size), :] = ref[...]
    token_ref[...] = jnp.zeros_like(token_ref)


def assemble(parts, after):
    size = parts[0].shape[0]
    return pl.pallas_call(
        assemble_kernel,
        in_specs=[VMEM] * 4 + [ANY],
        out_specs=[VMEM] * 2,
        out_shape=[
            jax.ShapeDtypeStruct((4 * size, D), bf16),
            jax.ShapeDtypeStruct((8, 128), f32),
        ],
        compiler_params=params(8),
        cost_estimate=cost(0, size * D * 16),
    )(*parts, after)


def chunk_places(y):
    return [pl.ds(pl.multiple_of(lax.rem(y + chunk, 4) * 256, 256), 256) for chunk in range(4)]


def exp_kernel(away, own_ref, mate_ref, f0, f1, f2, f3, labels_ref, *refs):
    exp_ref, sums_ref = refs[-2:]
    core = here("core")
    first = (here("y") * 16 + here("z") * 4 + lax.rem(here("x") + away, 4)) * 2
    places = chunk_places(here("y"))
    totals = [None] * 8
    at_targets = [None] * 8
    for part, (rows_ref, shard) in enumerate(((own_ref, first + core), (mate_ref, first + 1 - core))):
        base = (shard * CLS_DEV).astype(f32)
        tail = rows_ref[SAMPLE:MSG, 0:128].astype(f32)
        columns = []
        for b in range(6):
            ids = tail[b : b + 1] * 64.0 + tail[6 + b : 7 + b] + base
            columns.append(jnp.broadcast_to(ids, (128, 128)).T)
        for quarter in range(8):
            row, chunk = (quarter // 4) * HALF, quarter % 4
            cosine = lax.dot_general(
                rows_ref[row : row + HALF, :],
                (f0, f1, f2, f3)[chunk][...],
                (((1,), (1,)), ((), ())),
                preferred_element_type=f32,
            )
            labels = labels_ref[0:1, places[chunk]]
            for half in range(2):
                lane = chunk * 2 + half
                lanes = slice(lane * 128, lane * 128 + 128)
                wanted = labels[:, half * 128 : half * 128 + 128]
                total, at_target = totals[lane], at_targets[lane]
                for b in range(3):
                    cos = cosine[b * 128 : b * 128 + 128, half * 128 : half * 128 + 128]
                    hit = columns[row // 128 + b] == wanted
                    expo = jnp.where(hit, 0.0, jnp.exp2(cos * exp2_scale))
                    at = part * SAMPLE + row + b * 128
                    exp_ref[at : at + 128, lanes] = expo.astype(bf16)
                    expo = jnp.sum(expo.reshape(16, 8, 128), axis=0)
                    chosen = jnp.sum(jnp.where(hit, cos, 0.0).reshape(16, 8, 128), axis=0)
                    total = expo if total is None else total + expo
                    at_target = chosen if at_target is None else at_target + chosen
                totals[lane], at_targets[lane] = total, at_target
    for chunk in range(4):
        for row, found in ((0, totals), (1, at_targets)):
            both = jnp.concatenate([found[2 * chunk], found[2 * chunk + 1]], axis=1)
            value = jnp.sum(both, axis=0, keepdims=True)
            if away:
                value = value + refs[0][row : row + 1, places[chunk]]
            sums_ref[row : row + 1, places[chunk]] = value


def exp_block(away, rows, faces, labels, *before):
    return pl.pallas_call(
        functools.partial(exp_kernel, away),
        in_specs=[VMEM] * (7 + len(before)),
        out_specs=[VMEM] * 2,
        out_shape=[
            jax.ShapeDtypeStruct((2 * SAMPLE, FACES), bf16),
            jax.ShapeDtypeStruct((2, FACES), f32),
        ],
        compiler_params=params(8),
        cost_estimate=cost(0, 0),
    )(*rows, *faces, labels, *before)


def coefficients(sums_ref, weight_ref):
    others = sums_ref[0:1, :]
    cos_t = sums_ref[1:2, :]
    sine_root = jnp.sqrt(1.001 - cos_t * cos_t)
    logit_t = logit_scale * (cos_t * cos_margin - sine_root * sin_margin)
    scaled = weight_ref[...] / (others + jnp.exp(logit_t))
    slope = logit_scale * (cos_margin + sin_margin * cos_t / sine_root)
    return scaled * logit_scale, -scaled * others * slope


def sum_kernel(exp_ref, own_ref, mate_ref, *refs):
    sum_ref, target_ref, mark_ref = refs[-3:]
    over_rows = (((0,), (0,)), ((), ()))
    for chunk in range(2):
        lanes = slice(chunk * 512, chunk * 512 + 512)
        summed, chosen = (ref[:, lanes] for ref in refs[:2]) if len(refs) > 3 else (None, None)
        for part, rows_ref in enumerate((own_ref, mate_ref)):
            expo = exp_ref[part * SAMPLE : part * SAMPLE + SAMPLE, lanes]
            mark_ref[part] = jnp.where(expo.astype(f32) == 0.0, 1.0, 0.0).astype(bf16)
            rows = rows_ref[0:SAMPLE, :]
            term = lax.dot_general(rows, expo, over_rows, preferred_element_type=f32)
            summed = term if summed is None else summed + term
            term = lax.dot_general(rows, mark_ref[part], over_rows, preferred_element_type=f32)
            chosen = term if chosen is None else chosen + term
        sum_ref[:, lanes] = summed
        target_ref[:, lanes] = chosen


def sum_block(expo, rows, before, *after):
    def kernel(*refs):
        n = 3 + len(before)
        sum_kernel(*refs[:n], *refs[n + len(after) :])

    return pl.pallas_call(
        kernel,
        in_specs=[VMEM] * (3 + len(before)) + [ANY] * len(after),
        out_specs=[VMEM] * 2,
        out_shape=[jax.ShapeDtypeStruct((D, FACES), f32)] * 2,
        scratch_shapes=[pltpu.VMEM((2, SAMPLE, 512), bf16)],
        compiler_params=params(12),
        cost_estimate=cost(4 * 4 * HALF * FACES * D, 6 * 1024 * 1024),
    )(expo, *rows, *before, *after)


def face_sum_kernel(sum_ref, target_ref, sums_ref, weight_ref, *refs):
    coef_ref = refs[-1]
    coef_ref[0:1, :], coef_ref[1:2, :] = coefficients(sums_ref, weight_ref)
    for chunk, place in enumerate(chunk_places(here("y"))):
        lanes = slice(chunk * 256, chunk * 256 + 256)
        value = sum_ref[:, lanes] * coef_ref[0:1, place] + target_ref[:, lanes] * coef_ref[1:2, place]
        refs[chunk - 5][...] = value.T.astype(bf16)


def face_sums(summed, chosen, sums, weight, *after):
    return pl.pallas_call(
        face_sum_kernel,
        in_specs=[VMEM] * 4 + [ANY] * len(after),
        out_specs=[VMEM] * 4,
        out_shape=[jax.ShapeDtypeStruct((256, D), bf16)] * 4,
        scratch_shapes=[pltpu.VMEM((2, FACES), f32)],
        compiler_params=params(8),
        cost_estimate=cost(0, 0),
    )(summed, chosen, sums, weight, *after)


def grad_kernel(exp_ref, f0, f1, f2, f3, sums_ref, weight_ref, *refs):
    cg_own_ref, cg_mate_ref, coef_ref, dcos_ref = refs[-4:]
    coef_ref[0:1, :], coef_ref[1:2, :] = coefficients(sums_ref, weight_ref)
    places = chunk_places(here("y"))
    coef = [coef_ref[0:1, place] for place in places]
    target_coef = [coef_ref[1:2, place] for place in places]
    for part, cg_ref in ((1, cg_mate_ref), (0, cg_own_ref)):
        rows = slice(part * SAMPLE, part * SAMPLE + SAMPLE)
        for chunk in range(4):
            lanes = slice(chunk * 256, chunk * 256 + 256)
            expo = exp_ref[rows, lanes].astype(f32)
            dcos_ref[part, :, lanes] = jnp.where(
                expo == 0.0, target_coef[chunk], expo * coef[chunk]
            ).astype(bf16)
        grad = None
        for chunk, faces_ref in enumerate((f0, f1, f2, f3)):
            lanes = slice(chunk * 256, chunk * 256 + 256)
            term = jnp.dot(dcos_ref[part, :, lanes], faces_ref[...], preferred_element_type=f32)
            grad = term if grad is None else grad + term
        cg_ref[...] = grad.astype(bf16)


def grad_block(expo, faces, sums, weight, *after):
    return pl.pallas_call(
        grad_kernel,
        in_specs=[VMEM] * 7 + [ANY] * len(after),
        out_specs=[VMEM] * 2,
        out_shape=[jax.ShapeDtypeStruct((SAMPLE, D), bf16)] * 2,
        scratch_shapes=[
            pltpu.VMEM((2, FACES), f32),
            pltpu.VMEM((2, SAMPLE, FACES), bf16),
        ],
        compiler_params=params(10),
        cost_estimate=cost(0, 0),
    )(expo, *faces, sums, weight, *after)


def join_kernel(at, own_ref, mate_ref, *refs):
    out_ref = refs[-1]
    for half in range(2):
        rows = slice(half * HALF, half * HALF + HALF)
        value = own_ref[rows, :].astype(f32) + mate_ref[rows, :].astype(f32)
        if at == half:
            value = value + refs[0][...].astype(f32)
        out_ref[rows, :] = value.astype(bf16)


def join(cg, from_mate, at, arrived, *after):
    return pl.pallas_call(
        functools.partial(join_kernel, at),
        in_specs=[VMEM] * 3 + [ANY] * len(after),
        out_specs=VMEM,
        out_shape=jax.ShapeDtypeStruct((SAMPLE, D), bf16),
        compiler_params=params(8),
        cost_estimate=cost(SAMPLE * D * 2, SAMPLE * D * 6),
    )(cg, from_mate, arrived, *after)


def join_halves_kernel(own_ref, mate_ref, *refs):
    for half, out_ref in enumerate(refs[-2:]):
        rows = slice(half * HALF, half * HALF + HALF)
        out_ref[...] = (own_ref[rows, :].astype(f32) + mate_ref[rows, :].astype(f32)).astype(bf16)


def join_halves(cg, from_mate, *after):
    return pl.pallas_call(
        join_halves_kernel,
        in_specs=[VMEM] * 2 + [ANY] * len(after),
        out_specs=[VMEM] * 2,
        out_shape=[jax.ShapeDtypeStruct((HALF, D), bf16)] * 2,
        compiler_params=params(8),
        cost_estimate=cost(SAMPLE * D * 2, SAMPLE * D * 6),
    )(cg, from_mate, *after)


def rows_base_kernel(picked_ref, mom_ref, base_ref, inverse_ref):
    base_ref[...] = momentum_rate * mom_ref[...].astype(f32)
    inverse_ref[...] = inverse_norm(picked_ref[...].astype(f32))


def rows_base(*arrays):
    return pl.pallas_call(
        rows_base_kernel,
        in_specs=[VMEM] * 2,
        out_specs=[VMEM] * 2,
        out_shape=[
            jax.ShapeDtypeStruct((SAMPLE, D), f32),
            jax.ShapeDtypeStruct((SAMPLE, 1), f32),
        ],
        compiler_params=params(8),
        cost_estimate=cost(SAMPLE * D * 20, SAMPLE * D * 16),
    )(*arrays)


def rows_end_kernel(picked_ref, base_ref, inverse_ref, own_ref, mate_ref, v0_ref, v1_ref, velocity_ref, new_ref, velocity_buf, new_buf, arrived_buf, in_sem, sem):
    places = [pl.ds(piece * 192, 192) for piece in range(4)]
    arrivals = [
        [
            pltpu.make_async_copy(
                ref.at[place, :], arrived_buf.at[i, place, :], in_sem.at[piece, i]
            )
            for i, ref in enumerate((picked_ref, v0_ref, v1_ref))
        ]
        for piece, place in enumerate(places)
    ]
    for pair in arrivals:
        for copy in pair:
            copy.start()
    copies = []
    for piece, place in enumerate(places):
        rows = slice(piece * 192, piece * 192 + 192)
        inverse = inverse_ref[rows, :]
        grad = own_ref[rows, :].astype(f32) + mate_ref[rows, :].astype(f32)
        for copy in arrivals[piece]:
            copy.wait()
        picked = arrived_buf[0, rows, :].astype(f32)
        grad = grad + arrived_buf[1, rows, :].astype(f32) + arrived_buf[2, rows, :].astype(f32)
        along = inverse * inverse * jnp.sum(picked * grad, axis=1, keepdims=True)
        row_grad = inverse * (grad - picked * along)
        velocity = base_ref[rows, :] + row_grad
        velocity_buf[rows, :] = velocity
        new_buf[rows, :] = (picked - learn_rate * velocity).astype(bf16)
        for i, (buf, ref) in enumerate(((velocity_buf, velocity_ref), (new_buf, new_ref))):
            copy = pltpu.make_async_copy(buf.at[place, :], ref.at[place, :], sem.at[piece, i])
            copy.start()
            copies.append(copy)
    for copy in copies:
        copy.wait()


def rows_end(*arrays):
    return pl.pallas_call(
        rows_end_kernel,
        in_specs=[HBM] + [VMEM] * 4 + [HBM] * 2,
        out_specs=[HBM] * 2,
        out_shape=[
            jax.ShapeDtypeStruct((SAMPLE, D), f32),
            jax.ShapeDtypeStruct((SAMPLE, D), bf16),
        ],
        scratch_shapes=[
            pltpu.VMEM((SAMPLE, D), f32),
            pltpu.VMEM((SAMPLE, D), bf16),
            pltpu.VMEM((3, SAMPLE, D), bf16),
            pltpu.SemaphoreType.DMA((4, 3)),
            pltpu.SemaphoreType.DMA((4, 2)),
        ],
        compiler_params=params(10),
        cost_estimate=cost(0, 0),
    )(*arrays)


def split_kernel(a_ref, b_ref, c_ref, d_ref, *refs):
    outs, buf, sem = refs[-6:-2], refs[-2], refs[-1]
    arrivals = [
        pltpu.make_async_copy(ref, buf.at[i], sem.at[i])
        for i, ref in enumerate((a_ref, b_ref, c_ref, d_ref))
    ]
    for copy in arrivals:
        copy.start()
    for copy in arrivals:
        copy.wait()
    for k, out_ref in enumerate(outs):
        rows = pl.ds(pl.multiple_of(lax.rem(here("z") + k, 4) * 64, 64), 64)
        out_ref[...] = (
            buf[0, rows, :].astype(f32)
            + buf[1, rows, :].astype(f32)
            + buf[2, rows, :].astype(f32)
            + buf[3, rows, :].astype(f32)
        ).astype(bf16)


def split(parts, *after):
    return pl.pallas_call(
        split_kernel,
        in_specs=[HBM] * (4 + len(after)),
        out_specs=[VMEM] * 4,
        out_shape=[jax.ShapeDtypeStruct((64, D), bf16)] * 4,
        scratch_shapes=[pltpu.VMEM((4, 256, D), bf16), pltpu.SemaphoreType.DMA((4,))],
        compiler_params=params(8),
        cost_estimate=cost(0, 0),
    )(*parts, *after)


def faces_end_kernel(emb_ref, sums_ref, a_ref, b_ref, c_ref, d_ref, *refs):
    out_ref = refs[-1]
    start = pl.multiple_of(here("core") * 64, 64)
    values = emb_ref[pl.ds(start, 64), :].astype(f32)
    inverse = inverse_norm(values)
    unit = values * inverse
    summed = (
        a_ref[...].astype(f32)
        + b_ref[...].astype(f32)
        + c_ref[...].astype(f32)
        + d_ref[...].astype(f32)
    )
    out_ref[0:64, :] = inverse * (summed - unit * jnp.sum(unit * summed, axis=1, keepdims=True))
    block = here("y") * 4 + here("z")
    lanes = pl.ds(pl.multiple_of(lax.div(block, 2) * 128, 128), 128)
    cos_t = sums_ref[1:2, lanes]
    sine_root = jnp.sqrt(1.001 - cos_t * cos_t)
    logit_t = logit_scale * (cos_t * cos_margin - sine_root * sin_margin)
    loss = jnp.log(sums_ref[0:1, lanes] + jnp.exp(logit_t)) - logit_t
    loss = jnp.where(lax.rem(block, 2) == 0, loss, pltpu.roll(loss, 64, 1))
    out_ref[64:72, :] = jnp.broadcast_to(jnp.concatenate([loss] * 4, axis=1), (8, D))


def faces_end(embeddings, sums, parts, *after):
    return pl.pallas_call(
        faces_end_kernel,
        in_specs=[VMEM] * 6 + [ANY] * len(after),
        out_specs=VMEM,
        out_shape=jax.ShapeDtypeStruct((72, D), f32),
        compiler_params=params(8),
        cost_estimate=cost(64 * D * 12, 64 * D * 16),
    )(embeddings, sums, *parts, *after)


def both_cores_kernel(half_ref, mate_ref, out_ref, loss_ref):
    core = here("core")
    out_ref[pl.ds(pl.multiple_of(core * 64, 64), 64), :] = half_ref[0:64, :]
    out_ref[pl.ds(pl.multiple_of(64 - core * 64, 64), 64), :] = mate_ref[0:64, :]
    lane = lax.broadcasted_iota(jnp.int32, (1, 128), 1)
    own, mate = half_ref[64:65, 0:128], mate_ref[64:65, 0:128]
    low = jnp.where(core == 0, own, mate)
    high = jnp.where(core == 0, mate, own)
    loss_ref[...] = jnp.where(lane < 64, low, pltpu.roll(high, 64, 1))


def both_cores(*arrays):
    return pl.pallas_call(
        both_cores_kernel,
        in_specs=[VMEM] * 2,
        out_specs=[VMEM] * 2,
        out_shape=[
            jax.ShapeDtypeStruct((128, D), f32),
            jax.ShapeDtypeStruct((1, 128), f32),
        ],
        compiler_params=params(8),
        cost_estimate=cost(0, 64 * D * 16),
    )(*arrays)


def shift(array, axis, k):
    return lax.ppermute(array, axis, [((i + k) % 4, i) for i in range(4)])


def swap(array):
    return lax.ppermute(array, "core", [(0, 1), (1, 0)])


def total(array, axis):
    return array + shift(array, axis, 2) + shift(array, axis, 1) + shift(array, axis, 3)


def gather_rows(array, ids):
    return lax.gather(
        array,
        ids[:, None],
        lax.GatherDimensionNumbers(
            offset_dims=(1,), collapsed_slice_dims=(0,), start_index_map=(0,)
        ),
        slice_sizes=(1, D),
        mode=lax.GatherScatterMode.PROMISE_IN_BOUNDS,
    )


def shards(embeddings, labels, centres, momentum, sample_rows, cotangent):
    picked = gather_rows(centres, sample_rows)
    message, unit, my_labels, weight = prepare(
        picked, sample_rows, embeddings, labels, cotangent
    )

    up = shift(message, "x", -1)
    down = shift(message, "x", 1)
    own_rows = [message, swap(message)]

    plane, token = assemble(
        [unit] + [shift(unit, "z", k) for k in (1, 2, 3)], own_rows[1]
    )
    y1, y3 = shift(plane, "y", 1), shift(plane, "y", 3)
    y2 = paste(shift(cut(y1, 0, 128), "y", 1), shift(cut(y3, 128, 128), "y", 3))
    faces = [plane, y1, y2, y3]

    up, down = tie(up, faces[1], faces[3]), tie(down, faces[1], faces[3])
    c0, d1 = cut(up, 0, HALF), cut(down, HALF, MSG - HALF)
    up, down = tie(up, c0, d1), tie(down, c0, d1)
    c0, d1 = shift(c0, "x", -1), shift(d1, "x", 1)

    expo = {}
    expo["own"], sums_own = exp_block(0, own_rows, faces, my_labels)
    up_rows = [up, swap(up)]
    expo["up"], sums_up = exp_block(3, up_rows, faces, my_labels, sums_own)
    down_rows = [down, swap(down)]
    expo["down"], sums_down = exp_block(1, down_rows, faces, my_labels, sums_up)
    far = paste(c0, d1, sums_up)
    far_rows = [far, swap(far)]
    expo["far"], sums = exp_block(2, far_rows, faces, my_labels, sums_down)
    face_sum = sum_block(expo["own"], own_rows, (), sums)
    sums = total(sums, "y")
    face_sum = sum_block(expo["up"], up_rows, face_sum, sums)
    sums = total(sums, "z")
    sums = tie(sums, face_sum[0])

    def grads(name, *after):
        return grad_block(expo[name], faces, sums, weight, *after)

    far_own, far_mate = grads("far")
    up_own, up_mate = grads("up", far_mate)
    far_mate, up_mate = swap(far_mate), swap(up_mate)
    down_own, down_mate = grads("down", up_own)
    t0, t1 = join_halves(far_own, far_mate, down_own)
    r0, r1 = shift(t0, "x", 1), shift(t1, "x", -1)
    down_mate = swap(down_mate)
    face_sum = sum_block(expo["down"], down_rows, face_sum, t0)
    face_sum = sum_block(expo["far"], far_rows, face_sum)
    parts = face_sums(*face_sum, sums, weight, up_mate, down_mate, t0)
    cg_own, cg_mate = grads("own", t0)
    sent = copied(weight, parts[0], cg_own)
    v_up = join(up_own, up_mate, 0, r0, sent)
    v_down = join(down_own, down_mate, 1, r1, sent)
    v0, v1 = shift(v_up, "x", 1), shift(v_down, "x", -1)

    mom_rows = gather_rows(momentum, copied(sample_rows, v_up, v_down))
    parts = split(
        [parts[0]] + [shift(parts[k], "y", -k) for k in (1, 2, 3)], mom_rows
    )
    cg_mate = swap(tie(cg_mate, parts[0]))
    parts = [parts[0]] + [shift(parts[k], "z", -k) for k in (1, 2, 3)]
    base, inverse = rows_base(picked, mom_rows)
    half = faces_end(embeddings, sums, parts, v0, v1, inverse)
    grad_embed, loss = both_cores(half, swap(half))

    velocity, new_rows = rows_end(picked, base, inverse, cg_own, cg_mate, v0, v1)
    return (loss.reshape(128), grad_embed, velocity, new_rows)


def solution(mesh):
    grid = Mesh(mesh.devices.reshape(4, 4, 4, 2), ("y", "z", "x", "core"))
    chips = ("y", "z", "x")
    devices = ("y", "z", "x", "core")
    return jax.shard_map(
        shards,
        mesh=grid,
        in_specs=(
            P(chips, None),
            P(),
            P(devices, None),
            P(devices, None),
            P(devices),
            P(),
        ),
        out_specs=(P(chips), P(chips, None), P(devices, None), P(devices, None)),
        check_vma=False,
    )
```
